128 devices in a mesh: section: 2 (over x_hi), tensor: 4 (over z), dp: 16 (over y, x_lo, core).
Axes of the slice: x: 4 (x_hi: 2, x_lo: 2; x = x_hi * 2 + x_lo), y: 4, z: 4, core: 2. Of those that a mesh axis runs over, the one named last changes fastest.
Arguments:
- embedded: bfloat16 [8192, 768], P('dp'), may hold values from -6 to 6
- expert_index: int32 [2, 8192, 1], P('section', 'dp'), may hold values from 0 to 1
- buckets: int32 [128, 128], replicated, may hold values from 0 to 31
- rel_bias: float32 [32, 12], P(None, 'tensor'), may hold values from -6 to 6
- gain_attn: float32 [2, 768], P('section'), may hold values from 0.5 to 1.5
- w_qkv: bfloat16 [2, 3, 768, 768], P('section', None, None, 'tensor'), may hold values from -0.21875 to 0.21875
- w_out: bfloat16 [2, 768, 768], P('section', 'tensor'), may hold values from -1.25 to 1.25
- gain_ffn: float32 [2, 768], P('section'), may hold values from 0.5 to 1.5
- w_router: bfloat16 [2, 768, 2], P('section'), may hold values from -0.15625 to 0.15625
- w_in: bfloat16 [2, 2, 768, 3072], P('section', None, None, 'tensor'), may hold values from -0.21875 to 0.21875
- w_down: bfloat16 [2, 2, 3072, 768], P('section', None, 'tensor'), may hold values from -0.21875 to 0.21875
- cotangent: bfloat16 [8192, 768], P('dp'), may hold values from -6 to 6
Outputs:
- hidden: float32 [2, 8192, 768], P('section', 'dp')
- grad_input: float32 [2, 8192, 768], P('section', 'dp')
- grad_rel_bias: float32 [32, 12], P(None, 'tensor')
- grad_gain_attn: float32 [2, 768], P('section')
- grad_qkv: float32 [2, 3, 768, 768], P('section', None, None, 'tensor')
- grad_out: float32 [2, 768, 768], P('section', 'tensor')
- grad_gain_ffn: float32 [2, 768], P('section')
- grad_router: float32 [2, 768, 2], P('section')
- grad_in: float32 [2, 2, 768, 3072], P('section', None, None, 'tensor')
- grad_down: float32 [2, 2, 3072, 768], P('section', None, 'tensor')
The draws below stay inside these ranges and needn't reach their ends.
Inputs may be any that keep to these rules, and one draw needn't show every extreme that they name: `expert_index`: each token's expert in each layer; every one of the 2 experts is chosen by some token. `buckets`: bucket of each pair of query and key positions within a sequence.
All inputs are finite; a program needn't handle non-finite values.
Results may differ from the reference program's by a relative error of at most 0.034.
Values may be sent and summed in bfloat16 or wider, within the bound.
A program may use at most 128 MiB of HBM per device.

```python
import jax
import jax.numpy as jnp
from jax import lax

D = 768
H = 12
DH = 64
FF = 3072
NB = 32
E = 2
SEQ = 128
LAYERS = 2
TOKENS = 8192


def with_ends(entries, own_key, smallest, top_value):
    shape = entries.shape
    index_at = [jax.random.randint(jax.random.fold_in(own_key, axis), (), 0, shape[axis]) for axis in range(len(shape))]
    entries = entries.at[tuple(index_at)].set(smallest)
    longest = shape.index(max(shape))
    index_at[longest] = (index_at[longest] + 1) % shape[longest]
    return entries.at[tuple(index_at)].set(top_value)


def level_of(own_key, dims, shards, low, high):
    def one(position, blocks):
        draws = jax.random.uniform(jax.random.fold_in(jax.random.fold_in(own_key, 6), position), (blocks,), jnp.float32, low / len(shards), high / len(shards))
        return jnp.repeat(jnp.exp(draws), dims[position] // blocks).reshape((-1,) + (1,) * (len(dims) - position - 1))

    loudness = one(*shards[0])
    for cut in shards[1:]:
        loudness = loudness * one(*cut)
    return loudness


def picks_of(rng, rows, count, top, lift):
    ranking = jax.random.permutation(jax.random.fold_in(rng, 1), count)
    boost = ranking
    for power in range(3):
        boost = boost * boost // count
    boost = boost * lift // count
    tickets = jax.random.randint(jax.random.fold_in(rng, 2), (rows, count), 0, 4096) + boost
    fixed_rows = jax.random.permutation(jax.random.fold_in(rng, 3), rows)[jnp.arange(count) % rows]
    tickets = jnp.where(jnp.arange(rows)[:, None] == fixed_rows[None, :], 1 << 14, tickets)
    score = tickets * count + jnp.arange(count)
    return lax.top_k(score.astype(jnp.int32), top)[1].astype(jnp.int32)


def centred(stream_key, shape, width, limit, split=(), held_as=jnp.bfloat16):
    entries = jax.random.normal(stream_key, shape, jnp.float32) * width
    if len(split) > 0:
        entries = level_of(stream_key, shape, split, -0.22, 0.18) * entries
    return jnp.clip(entries, min=-limit, max=limit).astype(held_as)


def setup_inputs(seed: int = 0) -> dict:
    key_of = jax.random.split(jax.random.key(seed), 13)
    return {
        "embedded": centred(key_of[0], (TOKENS, D), 1.0, 6.0, ((0, 16),)),
        "expert_index": picks_of(key_of[1], LAYERS * TOKENS, E, 1, 0).reshape((LAYERS, TOKENS, 1)),
        "buckets": with_ends(jax.random.randint(key_of[2], (SEQ, SEQ), 0, NB), jax.random.fold_in(key_of[2], 1), 0, NB - 1).astype(jnp.int32),
        "rel_bias": centred(key_of[3], (NB, H), 1.0, 6.0, ((1, 4),), jnp.float32),
        "gain_attn": jnp.clip(1.0 + 0.1 * jax.random.normal(key_of[4], (LAYERS, D), jnp.float32), 0.5, 1.5),
        "w_qkv": centred(key_of[5], (LAYERS, 3, D, H * DH), D ** -0.5, 0.21875, ((0, 2), (3, 4))),
        "w_out": centred(key_of[6], (LAYERS, H * DH, D), (H * DH // 32) ** -0.5, 1.25, ((0, 2), (1, 4))),
        "gain_ffn": jnp.clip(1.0 + 0.1 * jax.random.normal(key_of[7], (LAYERS, D), jnp.float32), 0.5, 1.5),
        "w_router": centred(key_of[8], (LAYERS, D, E), (2 * D) ** -0.5, 0.15625, ((0, 2),)),
        "w_in": centred(key_of[9], (LAYERS, E, D, FF), D ** -0.5, 0.21875, ((0, 2), (3, 4))),
        "w_down": centred(key_of[10], (LAYERS, E, FF, D), (FF // 4) ** -0.5, 0.21875, ((0, 2), (2, 4))),
        "cotangent": centred(key_of[11], (TOKENS, D), 1.0, 6.0, ((0, 16),)),
    }


@jax.custom_vjp
def low(v):
    return lax.optimization_barrier(v.astype(jnp.bfloat16)).astype(jnp.float32)

@jax.custom_vjp
def low_back(v):
    return v

def low_keep(v):
    return (low(v), None)

def low_pass(kept, grad):
    return (grad,)

def back_keep(v):
    return (v, None)

def back_low(kept, grad):
    return (low(grad),)
low.defvjp(low_keep, low_pass)
low_back.defvjp(back_keep, back_low)
eps_norm = 1e-06
score_scale = 0.125
exact_mode = lax.Precision.HIGHEST

def rms_apply(values, gain_vec):
    return values * lax.rsqrt(lax.optimization_barrier(jnp.mean(values * values, axis=-1, keepdims=True)) + eps_norm) * gain_vec

def softmax_rows(scores):
    shifted = scores - lax.optimization_barrier(jnp.max(scores, axis=-1, keepdims=True))
    powers = jnp.exp(shifted)
    return powers / lax.optimization_barrier(jnp.sum(powers, axis=-1, keepdims=True))

def encoder_layer(hidden, routes, bucket_onehot, bias_table, gain_attn, w_qkv, w_out, gain_ffn, w_router, w_in, w_down):
    batch_seqs, seq_len, model_width = hidden.shape
    head_count = bias_table.shape[1]
    normed = low(rms_apply(hidden, gain_attn))
    projected = low_back(low(jnp.einsum('bsd,kdc->kbsc', normed, w_qkv, precision=exact_mode)))
    head_size = projected.shape[-1] // head_count
    split_heads = projected.reshape(3, batch_seqs, seq_len, head_count, head_size)
    position_bias = jnp.einsum('nij,nh->hij', bucket_onehot, bias_table, precision=exact_mode)
    scores = jnp.einsum('bihc,bjhc->bhij', split_heads[0], split_heads[1], precision=exact_mode) * score_scale
    scores = low_back(scores + position_bias[None])
    weights_low = low(softmax_rows(scores))
    attended = jnp.einsum('bhij,bjhc->bihc', weights_low, split_heads[2], precision=exact_mode)
    attended = low_back(low(attended.reshape(batch_seqs, seq_len, head_count * head_size)))
    branch_attn = low_back(jnp.einsum('bsc,cd->bsd', attended, w_out, precision=exact_mode))
    middle = hidden + branch_attn
    normed_ffn = low(rms_apply(middle, gain_ffn))
    logits = jnp.einsum('bsd,de->bse', normed_ffn, w_router, precision=exact_mode)
    expert_count = w_router.shape[1]
    choose = (routes[..., None] == jnp.arange(expert_count, dtype=jnp.int32)).astype(jnp.float32)
    gate_value = lax.optimization_barrier(jnp.sum(softmax_rows(logits) * choose, axis=-1, keepdims=True))
    pre_act = low_back(jnp.einsum('bsd,edf->ebsf', normed_ffn, w_in, precision=exact_mode))
    activated = low(jax.nn.gelu(pre_act))
    expert_out = jnp.einsum('ebsf,efd->ebsd', activated, w_down, precision=exact_mode)
    combined = low_back(jnp.einsum('ebsd,bse->bsd', expert_out, choose, precision=exact_mode))
    return middle + gate_value * combined

def two_sections(x_val, probe, bias_table, gain_attn, w_qkv, w_out, gain_ffn, w_router, w_in, w_down, bucket_onehot, routes):
    first = encoder_layer(x_val, routes[0], bucket_onehot, bias_table, gain_attn[0], w_qkv[0], w_out[0], gain_ffn[0], w_router[0], w_in[0], w_down[0])
    passed = low_back(low(first)) + probe
    second = encoder_layer(passed, routes[1], bucket_onehot, bias_table, gain_attn[1], w_qkv[1], w_out[1], gain_ffn[1], w_router[1], w_in[1], w_down[1])
    return (first, second)

def reference(embedded, expert_index, buckets, rel_bias, gain_attn, w_qkv, w_out, gain_ffn, w_router, w_in, w_down, cotangent):
    seq_count = TOKENS // SEQ
    block_seqs = min(seq_count, max(1, 4096 // SEQ))
    block_count = seq_count // block_seqs
    bucket_onehot = (buckets[None] == jnp.arange(NB, dtype=jnp.int32)[:, None, None]).astype(jnp.float32)
    params = (rel_bias.astype(jnp.float32), gain_attn.astype(jnp.float32), w_qkv.astype(jnp.float32), w_out.astype(jnp.float32), gain_ffn.astype(jnp.float32), w_router.astype(jnp.float32), w_in.astype(jnp.float32), w_down.astype(jnp.float32))
    inputs_blk = embedded.astype(jnp.float32).reshape(block_count, block_seqs, SEQ, D)
    cot_blk = cotangent.astype(jnp.float32).reshape(block_count, block_seqs, SEQ, D)
    route_blk = expert_index[..., 0].reshape(LAYERS, block_count, block_seqs, SEQ).transpose(1, 0, 2, 3)

    def one_block(totals, pieces):
        x_piece, cot_piece, route_piece = pieces

        def wrapped(x_val, probe, bias_table, g_attn, wq_all, wo_all, g_ffn, wr_all, wi_all, wd_all):
            return two_sections(x_val, probe, bias_table, g_attn, wq_all, wo_all, g_ffn, wr_all, wi_all, wd_all, bucket_onehot, route_piece)
        outputs, pullback = jax.vjp(wrapped, x_piece, jnp.zeros_like(x_piece), *params)
        grads = pullback((jnp.zeros_like(outputs[0]), cot_piece))
        totals = tuple((running + extra for running, extra in zip(totals, grads[2:])))
        return (totals, (outputs[0], outputs[1], grads[0], grads[1]))
    init = tuple((jnp.zeros_like(member) for member in params))
    totals, stacked = lax.scan(one_block, init, (inputs_blk, cot_blk, route_blk))
    hidden_out = jnp.stack([stacked[0].reshape(TOKENS, D), stacked[1].reshape(TOKENS, D)])
    grad_in_out = jnp.stack([stacked[2].reshape(TOKENS, D), stacked[3].reshape(TOKENS, D)])
    return (hidden_out, grad_in_out, totals[0], totals[1], totals[2], totals[3], totals[4], totals[5], totals[6], totals[7])
```

```python
import functools

import jax
import jax.numpy as jnp
from jax import lax
from jax.experimental import pallas as pl
from jax.experimental.pallas import tpu as pltpu
from jax.sharding import PartitionSpec as P

BF = jnp.bfloat16
F32 = jnp.float32
EPS = 1e-06
ROOT = 0.7978845608028654
CUBE = 0.044715
PLACE = {2: 0, 1: 1, 3: 2, 0: 3}
COPIES = 160


def dot(a, b):
    return jnp.dot(a, b, preferred_element_type=F32)


def dot_nt(a, b):
    return lax.dot_general(a, b, (((1,), (1,)), ((), ())), preferred_element_type=F32)


def dot_tn(a, b):
    return lax.dot_general(a, b, (((0,), (0,)), ((), ())), preferred_element_type=F32)


def wide(v):
    return v.astype(F32)


def inverse_rms(values):
    return lax.rsqrt(jnp.mean(values * values, axis=-1, keepdims=True) + EPS)


class Links:
    def __init__(self, send_sems, recv_sems):
        self.send_sems, self.recv_sems = send_sems, recv_sems
        self.used = 0
        self.pending = []

    def copy(self, src, dst, device, landing=None):
        slot = self.used
        self.used += 1
        make = functools.partial(
            pltpu.make_async_remote_copy,
            src_ref=src,
            send_sem=self.send_sems.at[slot],
            recv_sem=self.recv_sems.at[slot],
            device_id=device,
            device_id_type=pl.DeviceIdType.MESH,
        )
        out = make(dst_ref=dst)
        arriving = out if landing is None else make(dst_ref=landing)
        return out, arriving

    def send(self, src, dst, device, landing=None):
        out, arriving = self.copy(src, dst, device, landing)
        out.start()
        self.pending.append(out)
        return arriving

    def drain(self):
        for out in self.pending:
            out.wait_send()
        self.pending = []


class Gather:
    def __init__(self, links, local, remote, right, left):
        self.links, self.local, self.remote = links, local, remote
        self.right, self.left = right, left

    def start(self):
        send, local, remote = self.links.send, self.local, self.remote
        self.a_right = send(local(0, 0), remote(0, 0, 1), self.right, local(3, 0))
        self.b_left = send(local(0, 1), remote(0, 1, -1), self.left, local(1, 1))
        self.b_right = send(local(0, 1), remote(0, 1, 1), self.right, local(3, 1))
        self.a_left = send(local(0, 0), remote(0, 0, -1), self.left, local(1, 0))

    def forward(self):
        send, local, remote = self.links.send, self.local, self.remote
        self.a_right.wait_recv()
        self.a_far = send(local(3, 0), remote(3, 0, 1), self.right, local(2, 0))
        self.b_left.wait_recv()
        self.b_far = send(local(1, 1), remote(1, 1, -1), self.left, local(2, 1))

    def finish_near(self):
        self.b_right.wait_recv()
        self.a_left.wait_recv()

    def finish_far(self):
        self.a_far.wait_recv()
        self.b_far.wait_recv()

    def finish(self):
        self.finish_near()
        self.finish_far()


class Scatter:
    def __init__(self, links, part, landed, summed, right, left):
        self.links, self.part, self.landed, self.summed = links, part, landed, summed
        self.right, self.left = right, left

    def start_far(self):
        send, part, landed = self.links.send, self.part, self.landed
        self.far_a = send(part(2, 0), landed.at[0], self.right)
        self.far_b = send(part(2, 1), landed.at[1], self.left)

    def start_right(self):
        self.near_b = self.links.send(self.part(1, 1), self.landed.at[2], self.right)

    def start_left(self):
        self.near_a = self.links.send(self.part(3, 0), self.landed.at[3], self.left)

    def relay(self):
        send, part, landed, summed = self.links.send, self.part, self.landed, self.summed
        self.far_a.wait_recv()
        summed[0] = (wide(landed[0]) + wide(part(1, 0)[...])).astype(BF)
        self.sum_a = send(summed.at[0], landed.at[4], self.right)
        self.far_b.wait_recv()
        summed[1] = (wide(landed[1]) + wide(part(3, 1)[...])).astype(BF)
        self.sum_b = send(summed.at[1], landed.at[5], self.left)

    def finish(self):
        for arriving in (self.near_b, self.near_a, self.sum_a, self.sum_b):
            arriving.wait_recv()
        landed, part = self.landed, self.part
        top = wide(part(0, 0)[...]) + wide(landed[3]) + wide(landed[4])
        bottom = wide(part(0, 1)[...]) + wide(landed[2]) + wide(landed[5])
        return top, bottom


def kernel(
    embedded,
    expert_index,
    buckets,
    rel_bias,
    gain_attn,
    w_qkv,
    w_out,
    gain_ffn,
    router,
    w_in,
    w_down,
    cotangent,
    out_hidden,
    out_input,
    out_ffn,
    out_attn,
    out_small,
    x_all,
    n_attn,
    heads,
    probs,
    bias,
    att_all,
    w_out_all,
    middle,
    n_ffn,
    gate,
    expert,
    act,
    slope,
    part_a,
    part_b,
    part_c,
    landed_z,
    summed_z,
    combined,
    hidden_low,
    grad_top,
    grad_comb,
    grad_pre,
    grad_branch,
    grad_mid,
    input_low,
    grad_heads,
    grad_proj,
    table_rows,
    ffn_grads,
    attn_grads,
    ffn_pair,
    attn_pair,
    ffn_landed,
    attn_landed,
    ffn_summed,
    attn_summed,
    ffn_cross,
    attn_cross,
    small,
    small_z,
    small_y,
    small_xc,
    small_s,
    send_sems,
    recv_sems,
):
    section, t, d = lax.axis_index("section"), lax.axis_index("tensor"), lax.axis_index("dp")
    y, xl, c = d // 4, (d // 2) % 2, d % 2
    ztx = lambda k: {"tensor": (t + k) % 4}
    ydx = lambda k: {"dp": (d + 4 * k) % 16}
    x_mate, c_mate = {"dp": d + 2 - 4 * xl}, {"dp": d + 1 - 2 * c}
    xc_mate = {"dp": d + 2 - 4 * xl + 1 - 2 * c}
    s_mate = {"section": 1 - section}
    links = Links(send_sems, recv_sems)
    first, second = section == 0, section == 1

    barrier = pltpu.get_barrier_semaphore()
    mates = [ztx(1), ztx(2), ztx(3), ydx(1), ydx(2), ydx(3), x_mate, c_mate, xc_mate, s_mate]
    for mate in mates:
        pl.semaphore_signal(barrier, inc=1, device_id=mate, device_id_type=pl.DeviceIdType.MESH)

    def block(ref, k, rows=128):
        return ref.at[pl.ds(PLACE[k] * rows, rows)]

    def halves(ref):
        return lambda k, half: ref.at[pl.ds(PLACE[k] * 128 + half * 64, 64)]

    def halves_far(ref):
        return lambda k, half, way: ref.at[pl.ds(PLACE[(k - way) % 4] * 128 + half * 64, 64)]

    def own_order(ref):
        return lambda k, half: ref.at[pl.ds(((t + k) % 4) * 128 + half * 64, 64)]

    def own_order_far(ref):
        return lambda k, half, way: own_order(ref)(k, half)

    def z_gather(local, remote):
        return Gather(links, local, remote, ztx(1), ztx(3))

    for k in range(4):
        rows = pl.ds(PLACE[k] * 128, 128)
        theirs = pl.ds(((t + k) % 4) * 128, 128)
        expert[rows, :] = (expert_index[theirs, :] == 0).astype(F32)

        @pl.when(first)
        def _():
            x_all[rows, :] = embedded[theirs, :]

        @pl.when(second)
        def _():
            grad_top[rows, :] = cotangent[theirs, :]

    w_out_all[0] = w_out[...]
    which = buckets[...]
    for h in range(3):
        bias[h] = jnp.zeros((128, 128), F32)

    def add_bias(b, carry):
        hit = which == b
        for h in range(3):
            bias[h] = jnp.where(hit, rel_bias[b, h], bias[h])
        return carry

    lax.fori_loop(0, 32, add_bias, 0)
    pl.semaphore_wait(barrier, len(mates))

    w_gather = z_gather(
        lambda k, half: w_out_all.at[k, pl.ds(half * 96, 96)],
        lambda k, half, way: w_out_all.at[(k - way) % 4, pl.ds(half * 96, 96)],
    )
    w_gather.start()

    hop_out, hop_in = links.copy(hidden_low, x_all.at[pl.ds(PLACE[0] * 128, 128)], s_mate)

    @pl.when(first)
    def _():
        w_gather_done = None

    w_gather.forward()

    x_gather = z_gather(halves(x_all), halves_far(x_all))
    x_links = Links(send_sems, recv_sems)
    x_links.used = links.used
    links.used += 6
    x_gather.links = x_links

    @pl.when(second)
    def _():
        hop_in.wait_recv()
        x_gather.start()
        x_gather.forward()
        x_gather.finish()
        x_links.drain()

    for pair in (1, 0):
        rows = pl.ds(pair * 256, 256)
        values = wide(x_all[rows, :])
        normed = (values * inverse_rms(values) * gain_attn[...]).astype(BF)
        n_attn[rows, :] = normed
        for k in range(3):
            projected = dot(normed, w_qkv[k]).astype(BF)
            for h in range(3):
                heads[3 * k + h, rows, :] = projected[:, h * 64 : (h + 1) * 64]

    att_near_right, att_near_left = {}, {}
    for k in (0, 2, 1, 3):
        rows = pl.ds(PLACE[k] * 128, 128)
        for h in range(3):
            scores = dot_nt(heads[h, rows, :], heads[3 + h, rows, :]) * 0.125 + bias[h]
            powers = jnp.exp(scores - jnp.max(scores, axis=-1, keepdims=True))
            weights = powers / jnp.sum(powers, axis=-1, keepdims=True)
            probs[3 * k + h] = weights
            att_all[0, k, :, h * 64 : (h + 1) * 64] = dot(
                weights.astype(BF), heads[6 + h, rows, :]
            ).astype(BF)
        att_near_right[k] = links.send(
            att_all.at[0, k], att_all.at[3, (k - 1) % 4], ztx(1), att_all.at[3, k]
        )
        att_near_left[k] = links.send(
            att_all.at[0, k], att_all.at[1, (k + 1) % 4], ztx(3), att_all.at[1, k]
        )
    att_far = []
    for k in (0, 2, 1, 3):
        if k in (0, 1):
            m = (k - 1) % 4
            att_near_right[k].wait_recv()
            att_far.append(
                links.send(
                    att_all.at[3, m],
                    att_all.at[2, (m - 1) % 4],
                    ztx(1),
                    att_all.at[2, (m - 1) % 4],
                )
            )
        else:
            m = (k + 1) % 4
            att_near_left[k].wait_recv()
            att_far.append(
                links.send(
                    att_all.at[1, m],
                    att_all.at[2, (m + 1) % 4],
                    ztx(3),
                    att_all.at[2, (m + 1) % 4],
                )
            )
    for k in (2, 3):
        att_near_right[k].wait_recv()
    for k in (0, 1):
        att_near_left[k].wait_recv()
    w_gather.finish()
    for arriving in att_far:
        arriving.wait_recv()

    ffn_scatter = Scatter(
        links, halves(part_a), landed_z.at[0], summed_z.at[0], ztx(1), ztx(3)
    )
    for pair, ks in ((0, (2, 1)), (1, (3, 0))):
        rows = pl.ds(pair * 256, 256)
        total = wide(x_all[rows, :])
        for source in range(4):
            joined = jnp.concatenate([att_all[source, ks[0]], att_all[source, ks[1]]], axis=0)
            total = total + dot(joined, w_out_all[source])
        middle[rows, :] = total
        normed = (total * inverse_rms(total) * gain_ffn[...]).astype(BF)
        n_ffn[rows, :] = normed
        normed_wide = wide(normed)
        chosen = expert[rows, :]
        logit_gap = jnp.sum(normed_wide * router[0:1, :], axis=-1, keepdims=True) - jnp.sum(
            normed_wide * router[1:2, :], axis=-1, keepdims=True
        )
        gate[rows, :] = 1.0 / (1.0 + jnp.exp(jnp.where(chosen > 0.5, -logit_gap, logit_gap)))
        pre = jnp.where(chosen > 0.5, dot(normed, w_in[0]), dot(normed, w_in[1]))
        bent = jnp.tanh(ROOT * (pre + CUBE * pre * pre * pre))
        active = 0.5 * pre * (1.0 + bent)
        slope[rows, :] = 0.5 * (1.0 + bent) + 0.5 * pre * (1.0 - bent * bent) * ROOT * (
            1.0 + 3.0 * CUBE * pre * pre
        )
        active_low = active.astype(BF)
        act[rows, :] = active_low
        down = jnp.where(chosen > 0.5, dot(active_low, w_down[0]), dot(active_low, w_down[1]))
        part_a[rows, :] = down.astype(BF)
        if pair == 0:
            ffn_scatter.start_far()
            ffn_scatter.start_right()
        else:
            ffn_scatter.start_left()

    own = pl.ds(PLACE[0] * 128, 128)
    hidden_gather = z_gather(own_order(out_hidden), own_order_far(out_hidden))

    def end_forward():
        ffn_scatter.relay()
        top, bottom = ffn_scatter.finish()
        combined[0:64, :] = top
        combined[64:128, :] = bottom
        hidden_low[...] = (middle[own, :] + gate[own, :] * combined[...]).astype(BF)

    end_forward()

    @pl.when(first)
    def _():
        hop_out.start()

    out_hidden[pl.ds(t * 128, 128), :] = hidden_low[...]
    hidden_gather.start()
    hidden_gather.forward()

    back_out, back_in = links.copy(input_low, grad_top.at[pl.ds(PLACE[0] * 128, 128)], s_mate)
    top_gather = z_gather(halves(grad_top), halves_far(grad_top))
    top_links = Links(send_sems, recv_sems)
    top_links.used = links.used
    links.used += 6
    top_gather.links = top_links

    @pl.when(first)
    def _():
        hop_out.wait_send()
        back_in.wait_recv()
        top_gather.start()
        top_gather.forward()
        top_gather.finish()
        top_links.drain()

    back_scatter = Scatter(
        links, halves(part_b), landed_z.at[1], summed_z.at[1], ztx(1), ztx(3)
    )
    for pair in range(2):
        rows = pl.ds(pair * 256, 256)
        chosen = expert[rows, :]
        low = (gate[rows, :] * wide(grad_top[rows, :])).astype(BF)
        grad_comb[rows, :] = low
        into = jnp.where(chosen > 0.5, dot_nt(low, w_down[0]), dot_nt(low, w_down[1]))
        pre_low = (into * slope[rows, :]).astype(BF)
        grad_pre[rows, :] = pre_low
        back = jnp.where(chosen > 0.5, dot_nt(pre_low, w_in[0]), dot_nt(pre_low, w_in[1]))
        part_b[rows, :] = back.astype(BF)
        if pair == 0:
            back_scatter.start_far()
            back_scatter.start_right()
        else:
            back_scatter.start_left()
    back_scatter.relay()

    chosen_low = expert[...].astype(BF)
    other_low = (1.0 - expert[...]).astype(BF)
    for e, mask in enumerate((chosen_low, other_low)):
        ffn_grads[pl.ds(e * 768, 768), :] = dot_tn(n_ffn[...], grad_pre[...] * mask).astype(BF)
        ffn_grads[pl.ds(1536 + e * 768, 768), :] = dot_tn(act[...], grad_comb[...] * mask).astype(
            BF
        )

    class Reduce:
        def __init__(self, grads, pair_buf, landed, summed, cross, result):
            self.grads, self.pair_buf, self.cross, self.result = grads, pair_buf, cross, result
            rows = grads.shape[0]
            self.half, self.eighth, self.sixteenth = rows // 2, rows // 8, rows // 16
            self.scatter = Scatter(links, self.at(grads), landed, summed, ydx(1), ydx(3))
            local = self.at(result)
            self.gather = Gather(
                links, local, lambda k, half, way: local(k, half), ydx(1), ydx(3)
            )

        def at(self, ref):
            return lambda k, half: ref.at[
                pl.ds(
                    c * self.half + ((y + k) % 4) * self.eighth + half * self.sixteenth,
                    self.sixteenth,
                )
            ]

        def pair_start(self):
            theirs = self.grads.at[pl.ds((1 - c) * self.half, self.half)]
            self.paired = links.send(theirs, self.pair_buf, c_mate)

        def pair_finish(self):
            self.paired.wait_recv()
            step = 96

            def add(i, carry):
                mine = pl.ds(c * self.half + i * step, step)
                self.grads[mine, :] = (
                    wide(self.grads[mine, :]) + wide(self.pair_buf[pl.ds(i * step, step), :])
                ).astype(BF)
                return carry

            lax.fori_loop(0, self.half // step, add, 0)
            self.scatter.start_far()
            self.scatter.start_right()
            self.scatter.start_left()

        def relay(self):
            self.scatter.relay()

        def cross_start(self):
            top, bottom = self.scatter.finish()
            self.cross[0, 0 : self.sixteenth, :] = top.astype(BF)
            self.cross[0, self.sixteenth : self.eighth, :] = bottom.astype(BF)
            self.crossed = links.send(self.cross.at[0], self.cross.at[1], x_mate)

        def cross_finish(self):
            self.crossed.wait_recv()
            here = pl.ds(c * self.half + y * self.eighth, self.eighth)
            self.result[here, :] = (wide(self.cross[0]) + wide(self.cross[1])).astype(BF)
            self.gather.start()

        def forward(self):
            self.gather.forward()

        def share(self):
            self.gather.finish()
            mine = self.result.at[pl.ds(c * self.half, self.half)]
            theirs = self.result.at[pl.ds((1 - c) * self.half, self.half)]
            self.shared = links.send(mine, mine, c_mate, theirs)

        def finish(self):
            self.shared.wait_recv()

    ffn_sum = Reduce(ffn_grads, ffn_pair, ffn_landed, ffn_summed, ffn_cross, out_ffn)
    attn_sum = Reduce(attn_grads, attn_pair, attn_landed, attn_summed, attn_cross, out_attn)
    ffn_sum.pair_start()

    top, bottom = back_scatter.finish()
    from_units = jnp.concatenate([top, bottom], axis=0)
    top_own = wide(grad_top[own, :])
    grad_gate = jnp.sum(top_own * combined[...], axis=-1, keepdims=True)
    normed_own = wide(n_ffn[own, :])
    is_zero, gate_own = expert[own, :], gate[own, :]
    prob_zero = jnp.where(is_zero > 0.5, gate_own, 1.0 - gate_own)
    logit_zero = prob_zero * (is_zero - gate_own) * grad_gate
    logit_one = (1.0 - prob_zero) * (1.0 - is_zero - gate_own) * grad_gate
    small[...] = jnp.zeros_like(small)
    small[2:3, 0:768] = jnp.sum(normed_own * logit_zero, axis=0, keepdims=True)
    small[3:4, 0:768] = jnp.sum(normed_own * logit_one, axis=0, keepdims=True)
    grad_nffn = from_units + logit_zero * router[0:1, :] + logit_one * router[1:2, :]
    middle_own = middle[own, :]
    scale = inverse_rms(middle_own)
    small[1:2, 0:768] = jnp.sum(grad_nffn * middle_own * scale, axis=0, keepdims=True)
    g = grad_nffn * gain_ffn[...]
    inner = jnp.mean(g * middle_own, axis=-1, keepdims=True)
    grad_middle = top_own + scale * (g - middle_own * scale * scale * inner)
    grad_mid[...] = grad_middle
    grad_branch[own, :] = grad_middle.astype(BF)
    branch_gather = z_gather(halves(grad_branch), halves_far(grad_branch))
    branch_gather.start()
    ffn_sum.pair_finish()
    branch_gather.forward()
    branch_gather.finish()

    for pair in range(2):
        rows = pl.ds(pair * 256, 256)
        grad_att = dot_nt(grad_branch[rows, :], w_out[...]).astype(BF)
        for h in range(3):
            grad_heads[h, rows, :] = grad_att[:, h * 64 : (h + 1) * 64]
    table_rows[...] = jnp.zeros_like(table_rows)
    bias[...] = jnp.zeros_like(bias)
    attn_scatter = Scatter(
        links, halves(part_c), landed_z.at[2], summed_z.at[2], ztx(1), ztx(3)
    )
    for pair, ks in ((0, (2, 1)), (1, (3, 0))):
        for k in ks:
            rows = pl.ds(PLACE[k] * 128, 128)
            for h in range(3):
                weights = probs[3 * k + h]
                grad_att = grad_heads[h, rows, :]
                grad_w = dot_nt(grad_att, heads[6 + h, rows, :])
                mean = jnp.sum(weights * grad_w, axis=-1, keepdims=True)
                low = (weights * (grad_w - mean)).astype(BF)
                bias[h] += wide(low)
                at = h * 64
                grad_proj[rows, at : at + 64] = (0.125 * dot(low, heads[3 + h, rows, :])).astype(BF)
                at = 192 + h * 64
                grad_proj[rows, at : at + 64] = (0.125 * dot_tn(low, heads[h, rows, :])).astype(BF)
                at = 384 + h * 64
                grad_proj[rows, at : at + 64] = dot_tn(weights.astype(BF), grad_att).astype(BF)
        rows = pl.ds(pair * 256, 256)
        back = dot_nt(grad_proj[rows, 0:192], w_qkv[0])
        for k in range(1, 3):
            back = back + dot_nt(grad_proj[rows, k * 192 : (k + 1) * 192], w_qkv[k])
        part_c[rows, :] = back.astype(BF)
        if pair == 0:
            attn_scatter.start_far()
            attn_scatter.start_right()
        else:
            attn_scatter.start_left()
    attn_scatter.relay()
    ffn_sum.relay()

    attn_grads[0:576, :] = dot_tn(grad_proj[...], n_attn[...]).astype(BF)
    att_own = jnp.concatenate([att_all[0, k] for k in (2, 1, 3, 0)], axis=0)
    attn_grads[576:768, :] = dot_tn(att_own, grad_branch[...]).astype(BF)
    attn_sum.pair_start()

    top, bottom = attn_scatter.finish()
    grad_nattn = jnp.concatenate([top, bottom], axis=0)
    x_own = wide(x_all[own, :])
    scale = inverse_rms(x_own)
    small[0:1, 0:768] = jnp.sum(grad_nattn * x_own * scale, axis=0, keepdims=True)
    q = grad_nattn * gain_attn[...]
    inner = jnp.mean(q * x_own, axis=-1, keepdims=True)
    input_low[...] = (grad_mid[...] + scale * (q - x_own * scale * scale * inner)).astype(BF)

    @pl.when(second)
    def _():
        back_out.start()

    out_input[pl.ds(t * 128, 128), :] = input_low[...]
    input_gather = z_gather(own_order(out_input), own_order_far(out_input))
    input_gather.start()
    small_z[t] = small[:, 0:768]
    small_arrivals = [
        links.send(
            small.at[:, 0:768], small_z.at[t], ztx(k), small_z.at[(t + 4 - k) % 4]
        )
        for k in (1, 2, 3)
    ]
    attn_sum.pair_finish()
    ffn_sum.cross_start()

    def add_table(b, carry):
        hit = which == b
        for h in range(3):
            table_rows[h, pl.ds(b, 1), :] = jnp.sum(
                jnp.where(hit, bias[h], 0.0), axis=0, keepdims=True
            )
        return carry

    lax.fori_loop(0, 32, add_table, 0)
    ones = jnp.ones((8, 128), F32)
    for h in range(3):
        line = lax.dot_general(
            ones,
            table_rows[h],
            (((1,), (1,)), ((), ())),
            precision=lax.Precision.HIGHEST,
            preferred_element_type=F32,
        )
        small[h : h + 1, 768:896] = line[0:1, :]
    input_gather.forward()
    for arriving in small_arrivals:
        arriving.wait_recv()
    small_y[y, :, 0:768] = ((small_z[0] + small_z[1]) + small_z[2]) + small_z[3]
    small_y[y, :, 768:896] = small[:, 768:896]
    small_arrivals = [
        links.send(small_y.at[y], small_y.at[y], ydx(k), small_y.at[(y + 4 - k) % 4])
        for k in (1, 2, 3)
    ]
    attn_sum.relay()
    ffn_sum.cross_finish()
    for arriving in small_arrivals:
        arriving.wait_recv()
    place = 2 * xl + c
    small_xc[place] = ((small_y[0] + small_y[1]) + small_y[2]) + small_y[3]
    small_arrivals = [
        links.send(small_xc.at[place], small_xc.at[place], mate, small_xc.at[source])
        for mate, source in (
            (x_mate, 2 * (1 - xl) + c),
            (c_mate, 2 * xl + 1 - c),
            (xc_mate, 2 * (1 - xl) + 1 - c),
        )
    ]
    attn_sum.cross_start()
    ffn_sum.forward()
    attn_sum.cross_finish()
    for arriving in small_arrivals:
        arriving.wait_recv()
    total = ((small_xc[0] + small_xc[1]) + small_xc[2]) + small_xc[3]
    out_small[...] = total
    small_s[0] = total[:, 768:896]
    sections = links.send(small_s.at[0], small_s.at[1], s_mate)
    ffn_sum.share()
    attn_sum.forward()
    attn_sum.share()
    sections.wait_recv()
    out_small[:, 768:896] = small_s[0] + small_s[1]
    ffn_sum.finish()
    attn_sum.finish()
    hidden_gather.finish()
    input_gather.finish()

    @pl.when(second)
    def _():
        back_out.wait_send()

    links.drain()


def shards(
    embedded,
    expert_index,
    buckets,
    rel_bias,
    gain_attn,
    w_qkv,
    w_out,
    gain_ffn,
    w_router,
    w_in,
    w_down,
    cotangent,
):
    vmem, smem = pl.BlockSpec(memory_space=pltpu.VMEM), pl.BlockSpec(memory_space=pltpu.SMEM)
    hidden, grad_input, ffn, attn, small = pl.pallas_call(
        kernel,
        out_shape=[
            jax.ShapeDtypeStruct((512, 768), BF),
            jax.ShapeDtypeStruct((512, 768), BF),
            jax.ShapeDtypeStruct((3072, 768), BF),
            jax.ShapeDtypeStruct((768, 768), BF),
            jax.ShapeDtypeStruct((8, 896), F32),
        ],
        in_specs=[vmem, vmem, vmem, smem] + [vmem] * 8,
        out_specs=[vmem] * 5,
        scratch_shapes=[
            pltpu.VMEM((512, 768), BF),
            pltpu.VMEM((512, 768), BF),
            pltpu.VMEM((9, 512, 64), BF),
            pltpu.VMEM((12, 128, 128), F32),
            pltpu.VMEM((3, 128, 128), F32),
            pltpu.VMEM((4, 4, 128, 192), BF),
            pltpu.VMEM((4, 192, 768), BF),
            pltpu.VMEM((512, 768), F32),
            pltpu.VMEM((512, 768), BF),
            pltpu.VMEM((512, 1), F32),
            pltpu.VMEM((512, 1), F32),
            pltpu.VMEM((512, 768), BF),
            pltpu.VMEM((512, 768), F32),
            pltpu.VMEM((512, 768), BF),
            pltpu.VMEM((512, 768), BF),
            pltpu.VMEM((512, 768), BF),
            pltpu.VMEM((3, 6, 64, 768), BF),
            pltpu.VMEM((3, 2, 64, 768), BF),
            pltpu.VMEM((128, 768), F32),
            pltpu.VMEM((128, 768), BF),
            pltpu.VMEM((512, 768), BF),
            pltpu.VMEM((512, 768), BF),
            pltpu.VMEM((512, 768), BF),
            pltpu.VMEM((512, 768), BF),
            pltpu.VMEM((128, 768), F32),
            pltpu.VMEM((128, 768), BF),
            pltpu.VMEM((3, 512, 64), BF),
            pltpu.VMEM((512, 576), BF),
            pltpu.VMEM((3, 128, 128), F32),
            pltpu.VMEM((3072, 768), BF),
            pltpu.VMEM((768, 768), BF),
            pltpu.VMEM((1536, 768), BF),
            pltpu.VMEM((384, 768), BF),
            pltpu.VMEM((6, 192, 768), BF),
            pltpu.VMEM((6, 48, 768), BF),
            pltpu.VMEM((2, 192, 768), BF),
            pltpu.VMEM((2, 48, 768), BF),
            pltpu.VMEM((2, 384, 768), BF),
            pltpu.VMEM((2, 96, 768), BF),
            pltpu.VMEM((8, 896), F32),
            pltpu.VMEM((4, 8, 768), F32),
            pltpu.VMEM((4, 8, 896), F32),
            pltpu.VMEM((4, 8, 896), F32),
            pltpu.VMEM((2, 8, 128), F32),
            pltpu.SemaphoreType.DMA((COPIES,)),
            pltpu.SemaphoreType.DMA((COPIES,)),
        ],
        compiler_params=pltpu.CompilerParams(
            collective_id=0, has_side_effects=True, vmem_limit_bytes=60 * 1024 * 1024
        ),
    )(
        embedded,
        expert_index[0],
        buckets,
        rel_bias,
        gain_attn,
        w_qkv[0],
        w_out[0],
        gain_ffn,
        w_router[0].astype(F32).T,
        w_in[0],
        w_down[0],
        cotangent,
    )
    grad_qkv = jnp.transpose(attn[:576].reshape(3, 192, 768), (0, 2, 1)).astype(F32)
    ffn_wide = ffn.astype(F32)
    return (
        hidden.astype(F32)[None],
        grad_input.astype(F32)[None],
        small[0:3, 768:800].T,
        small[0:1, 0:768],
        grad_qkv[None],
        attn[576:].astype(F32)[None],
        small[1:2, 0:768],
        small[2:4, 0:768].T[None],
        ffn_wide[:1536].reshape(1, 2, 768, 768),
        ffn_wide[1536:].reshape(1, 2, 768, 768),
    )


def solution(mesh):
    in_specs = (
        P("dp", None),
        P("section", "dp", None),
        P(),
        P(None, "tensor"),
        P("section", None),
        P("section", None, None, "tensor"),
        P("section", "tensor", None),
        P("section", None),
        P("section", None, None),
        P("section", None, None, "tensor"),
        P("section", None, "tensor", None),
        P("dp", None),
    )
    out_specs = (
        P("section", "dp", None),
        P("section", "dp", None),
        P(None, "tensor"),
        P("section", None),
        P("section", None, None, "tensor"),
        P("section", "tensor", None),
        P("section", None),
        P("section", None, None),
        P("section", None, None, "tensor"),
        P("section", None, "tensor", None),
    )
    return jax.shard_map(shards, mesh=mesh, in_specs=in_specs, out_specs=out_specs, check_vma=False)
```

```python
import functools

import jax
import jax.numpy as jnp
from jax import lax
from jax.experimental import pallas as pl
from jax.experimental.pallas import tpu as pltpu
from jax.sharding import PartitionSpec as P

BF = jnp.bfloat16
F32 = jnp.float32
EPS = 1e-06
ROOT = 0.7978845608028654
CUBE = 0.044715
MB = 2
ROWS = 512 // MB
OWN = 128 // MB
HALF = OWN // 2
COPIES = 64 + 32 * MB


def dot(a, b):
    return jnp.dot(a, b, preferred_element_type=F32)


def dot_nt(a, b):
    return lax.dot_general(a, b, (((1,), (1,)), ((), ())), preferred_element_type=F32)


def dot_tn(a, b):
    return lax.dot_general(a, b, (((0,), (0,)), ((), ())), preferred_element_type=F32)


def wide(v):
    return v.astype(F32)


def inverse_rms(values):
    return lax.rsqrt(jnp.mean(values * values, axis=-1, keepdims=True) + EPS)


class Links:
    def __init__(self, send_sems, recv_sems):
        self.send_sems, self.recv_sems = send_sems, recv_sems
        self.used = 0
        self.pending = []

    def copy(self, src, dst, device, landing=None):
        return Copy(self, src, dst, device, landing)

    def drain(self):
        for out in self.pending:
            out.wait_send()
        self.pending = []


class Copy:
    def __init__(self, links, src, dst, device, landing):
        slot = links.used
        links.used += 1
        make = functools.partial(
            pltpu.make_async_remote_copy,
            src_ref=src,
            send_sem=links.send_sems.at[slot],
            recv_sem=links.recv_sems.at[slot],
            device_id=device,
            device_id_type=pl.DeviceIdType.MESH,
        )
        self.links = links
        self.out = make(dst_ref=dst)
        self.arriving = self.out if landing is None else make(dst_ref=landing)

    def start(self):
        self.out.start()
        self.links.pending.append(self.out)

    def wait(self):
        self.arriving.wait_recv()


class Gather:
    def __init__(self, links, at, right, left):
        copy = links.copy
        self.a_right = copy(at(0, 0), at(0, 0), right, at(3, 0))
        self.b_left = copy(at(0, 1), at(0, 1), left, at(1, 1))
        self.b_right = copy(at(0, 1), at(0, 1), right, at(3, 1))
        self.a_left = copy(at(0, 0), at(0, 0), left, at(1, 0))
        self.a_far = copy(at(3, 0), at(3, 0), right, at(2, 0))
        self.b_far = copy(at(1, 1), at(1, 1), left, at(2, 1))

    def start(self):
        for first in (self.a_right, self.b_left, self.b_right, self.a_left):
            first.start()

    def forward(self):
        self.a_right.wait()
        self.a_far.start()
        self.b_left.wait()
        self.b_far.start()

    def finish(self):
        for arriving in (self.b_right, self.a_left, self.a_far, self.b_far):
            arriving.wait()


class Scatter:
    def __init__(self, links, part, landed, summed, right, left):
        self.part, self.landed, self.summed = part, landed, summed
        copy = links.copy
        self.far_a = copy(part(2, 0), landed.at[0], right)
        self.far_b = copy(part(2, 1), landed.at[1], left)
        self.near_b = copy(part(1, 1), landed.at[2], right)
        self.near_a = copy(part(3, 0), landed.at[3], left)
        self.sum_a = copy(summed.at[0], landed.at[4], right)
        self.sum_b = copy(summed.at[1], landed.at[5], left)

    def start(self):
        for first in (self.far_a, self.far_b, self.near_b, self.near_a):
            first.start()

    def relay(self):
        part, landed, summed = self.part, self.landed, self.summed
        self.far_a.wait()
        summed[0] = (wide(landed[0]) + wide(part(1, 0)[...])).astype(BF)
        self.sum_a.start()
        self.far_b.wait()
        summed[1] = (wide(landed[1]) + wide(part(3, 1)[...])).astype(BF)
        self.sum_b.start()

    def finish(self):
        for arriving in (self.near_b, self.near_a, self.sum_a, self.sum_b):
            arriving.wait()
        landed, part = self.landed, self.part
        top = wide(part(0, 0)[...]) + wide(landed[3]) + wide(landed[4])
        bottom = wide(part(0, 1)[...]) + wide(landed[2]) + wide(landed[5])
        return jnp.concatenate([top, bottom], axis=0)


class DirectGather:
    def __init__(self, links, at, device):
        self.copies = [
            links.copy(at(0), at(0), device(k), at((4 - k) % 4)) for k in (2, 1, 3)
        ]

    def start(self):
        for out in self.copies:
            out.start()

    def forward(self):
        pass

    def finish(self):
        for arriving in self.copies:
            arriving.wait()


class DirectScatter:
    def __init__(self, links, part, landed, device):
        self.part, self.landed = part, landed
        self.copies = [
            links.copy(part(k), landed.at[i], device(k)) for i, k in enumerate((2, 1, 3))
        ]

    def start(self):
        for out in self.copies:
            out.start()

    def relay(self):
        pass

    def finish(self):
        for arriving in self.copies:
            arriving.wait()
        landed = self.landed
        return ((wide(self.part(0)[...]) + wide(landed[0])) + wide(landed[1])) + wide(landed[2])


class Reduce:
    def __init__(self, links, place, mates, grads, result, base, rows, pair, landed, summed, cross):
        (y, c), (ring, x_mate, c_mate) = place, mates
        self.grads, self.result, self.pair, self.cross = grads, result, pair, cross
        self.half, eighth, sixteenth = rows // 2, rows // 8, rows // 16
        self.mine = pl.multiple_of(base + c * self.half, 16)

        def at(ref):
            def view(k, half=None):
                start = self.mine + ((y + k) % 4) * eighth
                if half is None:
                    return ref.at[pl.ds(pl.multiple_of(start, 16), eighth)]
                start = start + half * sixteenth
                return ref.at[pl.ds(pl.multiple_of(start, 16), sixteenth)]

            return view

        theirs = pl.ds(pl.multiple_of(base + (1 - c) * self.half, 16), self.half)
        mine = pl.ds(self.mine, self.half)
        self.here = pl.ds(pl.multiple_of(self.mine + y * eighth, 16), eighth)
        self.paired = links.copy(grads.at[theirs], pair, c_mate)
        if summed is None:
            self.scatter = DirectScatter(links, at(grads), landed, ring)
        else:
            self.scatter = Scatter(links, at(grads), landed, summed, ring(1), ring(3))
        self.crossed = links.copy(cross.at[0], cross.at[1], x_mate)
        if summed is None:
            self.gather = DirectGather(links, at(result), ring)
        else:
            self.gather = Gather(links, at(result), ring(1), ring(3))
        self.shared = links.copy(result.at[mine], result.at[mine], c_mate, result.at[theirs])

    def pair_start(self):
        self.paired.start()

    def pair_finish(self):
        self.paired.wait()
        step = 96

        def add(i, carry):
            mine = pl.ds(pl.multiple_of(self.mine + i * step, 16), step)
            self.grads[mine, :] = (
                wide(self.grads[mine, :]) + wide(self.pair[pl.ds(i * step, step), :])
            ).astype(BF)
            return carry

        lax.fori_loop(0, self.half // step, add, 0)
        self.scatter.start()

    def relay(self):
        self.scatter.relay()

    def cross_start(self):
        self.cross[0] = self.scatter.finish().astype(BF)
        self.crossed.start()

    def cross_finish(self):
        self.crossed.wait()
        self.result[self.here, :] = (wide(self.cross[0]) + wide(self.cross[1])).astype(BF)
        self.gather.start()

    def forward(self):
        self.gather.forward()

    def share(self):
        self.gather.finish()
        self.shared.start()

    def finish(self):
        self.shared.wait()


def kernel(
    embedded,
    expert_index,
    buckets,
    rel_bias,
    gain_attn,
    w_qkv,
    w_out,
    gain_ffn,
    router,
    w_in_hbm,
    w_down_hbm,
    cotangent,
    out_hidden,
    out_input,
    out_ffn,
    out_attn,
    out_small,
    x_all,
    n_attn,
    heads,
    probs,
    bias,
    table_sums,
    att_all,
    w_out_all,
    middle,
    n_ffn,
    gate,
    expert,
    act,
    slope,
    part_a,
    part_b,
    part_c,
    landed_z,
    grad_top,
    grad_comb,
    grad_pre,
    grad_branch,
    grad_mid,
    grad_heads,
    grad_proj,
    table_rows,
    ffn_grads,
    attn_grads,
    ffn_pair,
    attn_pair,
    ffn_landed,
    attn_landed,
    ffn_summed,
    ffn_cross,
    attn_cross,
    small,
    small_z,
    small_y,
    small_xc,
    small_s,
    w_in,
    w_down,
    load_sems,
    send_sems,
    recv_sems,
):
    section, t, d = lax.axis_index("section"), lax.axis_index("tensor"), lax.axis_index("dp")
    y, xl, c = d // 4, (d // 2) % 2, d % 2
    ztx = lambda k: {"tensor": (t + k) % 4}
    ydx = lambda k: {"dp": (d + 4 * k) % 16}
    x_mate, c_mate = {"dp": d + 2 - 4 * xl}, {"dp": d + 1 - 2 * c}
    xc_mate = {"dp": d + 2 - 4 * xl + 1 - 2 * c}
    s_mate = {"section": 1 - section}
    links = Links(send_sems, recv_sems)

    load_in = pltpu.make_async_copy(w_in_hbm, w_in, load_sems.at[0])
    load_down = pltpu.make_async_copy(w_down_hbm, w_down, load_sems.at[1])
    load_embedded = pltpu.make_async_copy(embedded, x_all, load_sems.at[2])
    load_cotangent = pltpu.make_async_copy(cotangent, grad_top, load_sems.at[3])

    @pl.when(section == 0)
    def _():
        load_embedded.start()

    @pl.when(section == 1)
    def _():
        load_cotangent.start()

    load_in.start()
    load_down.start()
    barrier = pltpu.get_barrier_semaphore()
    mates = [ztx(1), ztx(2), ztx(3), ydx(1), ydx(2), ydx(3), x_mate, c_mate, xc_mate, s_mate]
    for mate in mates:
        pl.semaphore_signal(barrier, inc=1, device_id=mate, device_id_type=pl.DeviceIdType.MESH)

    def part_rows(m):
        return pl.ds(m * ROWS, ROWS)

    def own_rows(m):
        return pl.ds(pl.multiple_of(m * ROWS + t * OWN, OWN), OWN)

    def kept_rows(m):
        return pl.ds(m * OWN, OWN)

    def blocks(ref, m):
        return lambda k: ref.at[
            pl.ds(pl.multiple_of(m * ROWS + ((t + k) % 4) * OWN, OWN), OWN)
        ]

    def z_gather(at):
        return DirectGather(links, at, ztx)

    def z_scatter(part, kind, m):
        return DirectScatter(links, blocks(part, m), landed_z.at[kind, m], ztx)

    parts = range(MB)
    w_gather = z_gather(lambda k: w_out_all.at[(t + k) % 4])
    x_gather = [z_gather(blocks(x_all, m)) for m in parts]
    att_gather = [
        z_gather(lambda k, m=m: att_all.at[(t + k) % 4, pl.ds(m * ROWS, ROWS)])
        for m in parts
    ]
    ffn_scatter = [z_scatter(part_a, 0, m) for m in parts]
    hidden_gather = [z_gather(blocks(out_hidden, m)) for m in parts]
    top_gather = [z_gather(blocks(grad_top, m)) for m in parts]
    back_scatter = [z_scatter(part_b, 1, m) for m in parts]
    branch_gather = [z_gather(blocks(grad_branch, m)) for m in parts]
    attn_scatter = [z_scatter(part_c, 2, m) for m in parts]
    input_gather = [z_gather(blocks(out_input, m)) for m in parts]
    onward = [
        links.copy(out_hidden.at[own_rows(m)], x_all.at[own_rows(m)], s_mate) for m in parts
    ]
    returned = [
        links.copy(out_input.at[own_rows(m)], grad_top.at[own_rows(m)], s_mate) for m in parts
    ]
    place, ring = (y, c), (ydx, x_mate, c_mate)
    down_sum, in_sum = [
        Reduce(
            links,
            place,
            ring,
            ffn_grads,
            out_ffn,
            1536 * (1 - i),
            1536,
            ffn_pair.at[i],
            ffn_landed.at[i],
            ffn_summed.at[i],
            ffn_cross.at[i],
        )
        for i in range(2)
    ]
    attn_sum = Reduce(
        links,
        place,
        ring,
        attn_grads,
        out_attn,
        0,
        768,
        attn_pair,
        attn_landed,
        None,
        attn_cross,
    )
    small_over_z = [
        links.copy(small.at[:, 0:768], small_z.at[t], ztx(k), small_z.at[(t + 4 - k) % 4])
        for k in (1, 2, 3)
    ]
    small_over_y = [
        links.copy(small_y.at[y], small_y.at[y], ydx(k), small_y.at[(y + 4 - k) % 4])
        for k in (1, 2, 3)
    ]
    spot = 2 * xl + c
    small_over_xc = [
        links.copy(small_xc.at[spot], small_xc.at[spot], mate, small_xc.at[source])
        for mate, source in (
            (x_mate, 2 * (1 - xl) + c),
            (c_mate, 2 * xl + 1 - c),
            (xc_mate, 2 * (1 - xl) + 1 - c),
        )
    ]
    small_over_s = links.copy(small_s.at[0], small_s.at[1], s_mate)

    expert[...] = (expert_index[...] == 0).astype(F32)
    w_out_all[t] = w_out[...]
    small[...] = jnp.zeros_like(small)
    table_sums[...] = jnp.zeros_like(table_sums)
    bias[...] = jnp.zeros_like(bias)
    table_rows[...] = jnp.zeros_like(table_rows)

    def add_bias(b, carry):
        hit = buckets[...] == b
        for h in range(3):
            bias[h] = jnp.where(hit, rel_bias[b, h], bias[h])
        return carry

    lax.fori_loop(0, 32, add_bias, 0)

    def attention(m):
        rows = part_rows(m)
        values = wide(x_all[rows, :])
        normed = (values * inverse_rms(values) * gain_attn[...]).astype(BF)
        n_attn[rows, :] = normed
        for k in range(3):
            projected = dot(normed, w_qkv[k]).astype(BF)
            for h in range(3):
                heads[3 * k + h, rows, :] = projected[:, h * 64 : (h + 1) * 64]
        for s in range(m * ROWS // 128, (m + 1) * ROWS // 128):
            rows = pl.ds(s * 128, 128)
            for h in range(3):
                scores = dot_nt(heads[h, rows, :], heads[3 + h, rows, :]) * 0.125 + bias[h]
                powers = jnp.exp(scores - jnp.max(scores, axis=-1, keepdims=True))
                weights = powers / jnp.sum(powers, axis=-1, keepdims=True)
                probs[3 * s + h] = weights
                att_all[t, rows, h * 64 : (h + 1) * 64] = dot(
                    weights.astype(BF), heads[6 + h, rows, :]
                ).astype(BF)
        att_gather[m].start()

    def experts(m):
        rows = part_rows(m)
        att_gather[m].finish()
        total = wide(x_all[rows, :])
        for source in range(4):
            total = total + dot(att_all[source, rows, :], w_out_all[source])
        middle[rows, :] = total
        normed = (total * inverse_rms(total) * gain_ffn[...]).astype(BF)
        n_ffn[rows, :] = normed
        chosen = expert[rows, :]
        gap = jnp.sum(wide(normed) * (router[0:1, :] - router[1:2, :]), axis=-1, keepdims=True)
        gate[rows, :] = 1.0 / (1.0 + jnp.exp(jnp.where(chosen > 0.5, -gap, gap)))
        pre = jnp.where(chosen > 0.5, dot(normed, w_in[0]), dot(normed, w_in[1]))
        square = pre * pre
        bent = jnp.tanh(ROOT * pre * (1.0 + CUBE * square))
        active = 0.5 * pre * (1.0 + bent)
        slope[rows, :] = 0.5 * (1.0 + bent) + (0.5 * ROOT) * pre * (1.0 - bent * bent) * (
            1.0 + 3.0 * CUBE * square
        )
        active_low = active.astype(BF)
        act[rows, :] = active_low
        down = jnp.where(chosen > 0.5, dot(active_low, w_down[0]), dot(active_low, w_down[1]))
        part_a[rows, :] = down.astype(BF)

    def end_layer(m):
        combined = ffn_scatter[m].finish()
        own = own_rows(m)
        out_hidden[own, :] = (middle[own, :] + gate[own, :] * combined).astype(BF)

    def experts_back(m):
        rows = part_rows(m)
        chosen, share = expert[rows, :], gate[rows, :]
        top = wide(grad_top[rows, :])
        low = (share * top).astype(BF)
        grad_comb[rows, :] = low
        into = jnp.where(chosen > 0.5, dot_nt(low, w_down[0]), dot_nt(low, w_down[1]))
        pre_low = (into * slope[rows, :]).astype(BF)
        grad_pre[rows, :] = pre_low
        back = jnp.where(chosen > 0.5, dot_nt(pre_low, w_in[0]), dot_nt(pre_low, w_in[1]))
        grad_gate = jnp.sum(top * wide(part_a[rows, :]), axis=-1, keepdims=True)
        logit = share * (1.0 - share) * grad_gate * (2.0 * chosen - 1.0)
        small[0:1, 0:768] += jnp.sum(wide(n_ffn[rows, :]) * logit, axis=0, keepdims=True)
        part_b[rows, :] = (back + logit * (router[0:1, :] - router[1:2, :])).astype(BF)
        back_scatter[m].start()

    def middle_back(m):
        own = own_rows(m)
        grad_nffn = back_scatter[m].finish()
        values = middle[own, :]
        scale = inverse_rms(values)
        small[3:4, 0:768] += jnp.sum(grad_nffn * values * scale, axis=0, keepdims=True)
        g = grad_nffn * gain_ffn[...]
        inner = jnp.mean(g * values, axis=-1, keepdims=True)
        grad_middle = wide(grad_top[own, :]) + scale * (g - values * scale * scale * inner)
        grad_mid[kept_rows(m), :] = grad_middle
        grad_branch[own, :] = grad_middle.astype(BF)
        branch_gather[m].start()

    def attention_back(m):
        rows = part_rows(m)
        branch_gather[m].finish()
        grad_att = dot_nt(grad_branch[rows, :], w_out[...]).astype(BF)
        for h in range(3):
            grad_heads[h, rows, :] = grad_att[:, h * 64 : (h + 1) * 64]
        for s in range(m * ROWS // 128, (m + 1) * ROWS // 128):
            rows = pl.ds(s * 128, 128)
            for h in range(3):
                weights = probs[3 * s + h]
                grad_att = grad_heads[h, rows, :]
                grad_w = dot_nt(grad_att, heads[6 + h, rows, :])
                mean = jnp.sum(weights * grad_w, axis=-1, keepdims=True)
                low = (weights * (grad_w - mean)).astype(BF)
                table_sums[h] += wide(low)
                at = h * 64
                grad_proj[rows, at : at + 64] = (0.125 * dot(low, heads[3 + h, rows, :])).astype(BF)
                at = 192 + h * 64
                grad_proj[rows, at : at + 64] = (0.125 * dot_tn(low, heads[h, rows, :])).astype(BF)
                at = 384 + h * 64
                grad_proj[rows, at : at + 64] = dot_tn(weights.astype(BF), grad_att).astype(BF)
        rows = part_rows(m)
        back = dot_nt(grad_proj[rows, 0:192], w_qkv[0])
        for k in range(1, 3):
            back = back + dot_nt(grad_proj[rows, k * 192 : (k + 1) * 192], w_qkv[k])
        part_c[rows, :] = back.astype(BF)
        attn_scatter[m].start()

    def input_back(m):
        own = own_rows(m)
        grad_nattn = attn_scatter[m].finish()
        values = wide(x_all[own, :])
        scale = inverse_rms(values)
        small[2:3, 0:768] += jnp.sum(grad_nattn * values * scale, axis=0, keepdims=True)
        q = grad_nattn * gain_attn[...]
        inner = jnp.mean(q * values, axis=-1, keepdims=True)
        out_input[own, :] = (
            grad_mid[kept_rows(m), :] + scale * (q - values * scale * scale * inner)
        ).astype(BF)

    def expert_grads(base, left, right):
        for e in range(2):
            mask = expert[...] if e == 0 else 1.0 - expert[...]
            masked = right[...] * mask.astype(BF)
            ffn_grads[pl.ds(base + e * 768, 768), :] = dot_tn(left[...], masked).astype(BF)

    def down_grads():
        expert_grads(1536, act, grad_comb)
        down_sum.pair_start()

    def in_grads():
        expert_grads(0, n_ffn, grad_pre)
        in_sum.pair_start()

    def attention_grads():
        attn_grads[0:576, :] = dot_tn(grad_proj[...], n_attn[...]).astype(BF)
        attn_grads[576:768, :] = dot_tn(att_all[t], grad_branch[...]).astype(BF)
        attn_sum.pair_start()

    def small_z_start():
        small[1:2, 0:768] = -small[0:1, 0:768]
        small_z[t] = small[:, 0:768]
        for out in small_over_z:
            out.start()

    def table():
        def add_table(b, carry):
            hit = buckets[...] == b
            for h in range(3):
                table_rows[h, pl.ds(b, 1), :] = jnp.sum(
                    jnp.where(hit, table_sums[h], 0.0), axis=0, keepdims=True
                )
            return carry

        lax.fori_loop(0, 32, add_table, 0)
        for h in range(3):
            line = lax.dot_general(
                jnp.ones((8, 128), F32),
                table_rows[h],
                (((1,), (1,)), ((), ())),
                precision=lax.Precision.HIGHEST,
                preferred_element_type=F32,
            )
            small[h : h + 1, 768:896] = line[0:1, :]

    def small_y_start():
        for arriving in small_over_z:
            arriving.wait()
        small_y[y, :, 0:768] = ((small_z[0] + small_z[1]) + small_z[2]) + small_z[3]
        small_y[y, :, 768:896] = small[:, 768:896]
        for out in small_over_y:
            out.start()

    def small_xc_start():
        for arriving in small_over_y:
            arriving.wait()
        small_xc[spot] = ((small_y[0] + small_y[1]) + small_y[2]) + small_y[3]
        for out in small_over_xc:
            out.start()

    def small_s_start():
        for arriving in small_over_xc:
            arriving.wait()
        total = ((small_xc[0] + small_xc[1]) + small_xc[2]) + small_xc[3]
        out_small[...] = total
        small_s[0] = total[:, 768:896]
        small_over_s.start()

    def small_end():
        small_over_s.wait()
        out_small[:, 768:896] = small_s[0] + small_s[1]

    pl.semaphore_wait(barrier, len(mates))
    w_gather.start()
    opening = links.pending

    @pl.when(section == 0)
    def _():
        links.pending = list(opening)

        def middle_up(m):
            experts(m)
            ffn_scatter[m].start()

        def pass_on(m):
            end_layer(m)
            onward[m].start()
            hidden_gather[m].start()

        load_embedded.wait()
        attention(0)
        attention(1)
        w_gather.finish()
        load_in.wait()
        load_down.wait()
        middle_up(0)
        middle_up(1)
        pass_on(0)
        pass_on(1)
        for m in parts:
            returned[m].wait()
            top_gather[m].start()
        for m in parts:
            top_gather[m].finish()
            experts_back(m)
        down_grads()
        in_grads()
        middle_back(0)
        down_sum.pair_finish()
        middle_back(1)
        in_sum.pair_finish()
        attention_back(0)
        down_sum.relay()
        attention_back(1)
        attention_grads()
        in_sum.relay()
        table()
        input_back(0)
        input_gather[0].start()
        attn_sum.pair_finish()
        input_back(1)
        input_gather[1].start()
        small_z_start()
        down_sum.cross_start()
        in_sum.cross_start()
        attn_sum.cross_start()
        small_y_start()
        down_sum.cross_finish()
        in_sum.cross_finish()
        attn_sum.cross_finish()
        small_xc_start()
        down_sum.forward()
        in_sum.forward()
        small_s_start()
        attn_sum.share()
        down_sum.share()
        in_sum.share()
        small_end()
        for unit in (attn_sum, down_sum, in_sum):
            unit.finish()
        for m in parts:
            hidden_gather[m].finish()
            input_gather[m].finish()
        links.drain()

    @pl.when(section == 1)
    def _():
        links.pending = list(opening)
        load_cotangent.wait()
        load_in.wait()
        load_down.wait()
        w_gather.finish()
        for m in parts:
            onward[m].wait()
            x_gather[m].start()
        for m in parts:
            x_gather[m].finish()
            attention(m)
        for m in parts:
            experts(m)
            experts_back(m)
        for m in parts:
            middle_back(m)
        for m in parts:
            attention_back(m)
        for m in parts:
            input_back(m)
            returned[m].start()
        for m in parts:
            input_gather[m].start()
            ffn_scatter[m].start()
        down_grads()
        in_grads()
        attention_grads()
        down_sum.pair_finish()
        in_sum.pair_finish()
        attn_sum.pair_finish()
        small_z_start()
        table()
        for m in parts:
            end_layer(m)
            hidden_gather[m].start()
        small_y_start()
        small_xc_start()
        small_s_start()
        for step in ("relay", "cross_start", "cross_finish", "forward", "share", "finish"):
            for unit in (down_sum, in_sum, attn_sum):
                getattr(unit, step)()
        for m in parts:
            hidden_gather[m].finish()
            input_gather[m].finish()
        small_end()
        links.drain()


def widen(hidden, grad_input, ffn_in, ffn_down, attn, small, *outs):
    out_hidden, out_input, out_in, out_down, out_qkv, out_out = outs[:6]
    out_gain_attn, out_gain_ffn, out_router, out_table = outs[6:]
    out_hidden[...] = wide(hidden[...])
    out_input[...] = wide(grad_input[...])
    out_in[...] = wide(ffn_in[...])
    out_down[...] = wide(ffn_down[...])

    @pl.when(pl.program_id(0) == 0)
    def _():
        for k in range(3):
            out_qkv[k] = wide(attn[pl.ds(k * 192, 192), :]).T
        out_out[...] = wide(attn[pl.ds(576, 192), :])
        out_gain_attn[...] = small[2:3, 0:768]
        out_gain_ffn[...] = small[3:4, 0:768]
        out_router[...] = small[:, 0:768].T[:, 0:2]
        out_table[...] = small[:, 768:896].T[0:32, 0:3]


def shards(
    embedded,
    expert_index,
    buckets,
    rel_bias,
    gain_attn,
    w_qkv,
    w_out,
    gain_ffn,
    w_router,
    w_in,
    w_down,
    cotangent,
):
    vmem, smem = pl.BlockSpec(memory_space=pltpu.VMEM), pl.BlockSpec(memory_space=pltpu.SMEM)
    anywhere = pl.BlockSpec(memory_space=pl.ANY)
    hidden, grad_input, ffn, attn, small = pl.pallas_call(
        kernel,
        out_shape=[
            jax.ShapeDtypeStruct((512, 768), BF),
            jax.ShapeDtypeStruct((512, 768), BF),
            jax.ShapeDtypeStruct((3072, 768), BF),
            jax.ShapeDtypeStruct((768, 768), BF),
            jax.ShapeDtypeStruct((8, 896), F32),
        ],
        in_specs=[anywhere, vmem, vmem, smem] + [vmem] * 5 + [anywhere] * 3,
        out_specs=[vmem] * 5,
        scratch_shapes=[
            pltpu.VMEM((512, 768), BF),
            pltpu.VMEM((512, 768), BF),
            pltpu.VMEM((9, 512, 64), BF),
            pltpu.VMEM((12, 128, 128), F32),
            pltpu.VMEM((3, 128, 128), F32),
            pltpu.VMEM((3, 128, 128), F32),
            pltpu.VMEM((4, 512, 192), BF),
            pltpu.VMEM((4, 192, 768), BF),
            pltpu.VMEM((512, 768), F32),
            pltpu.VMEM((512, 768), BF),
            pltpu.VMEM((512, 1), F32),
            pltpu.VMEM((512, 1), F32),
            pltpu.VMEM((512, 768), BF),
            pltpu.VMEM((512, 768), F32),
            pltpu.VMEM((512, 768), BF),
            pltpu.VMEM((512, 768), BF),
            pltpu.VMEM((512, 768), BF),
            pltpu.VMEM((3, MB, 3, OWN, 768), BF),
            pltpu.VMEM((512, 768), BF),
            pltpu.VMEM((512, 768), BF),
            pltpu.VMEM((512, 768), BF),
            pltpu.VMEM((512, 768), BF),
            pltpu.VMEM((128, 768), F32),
            pltpu.VMEM((3, 512, 64), BF),
            pltpu.VMEM((512, 576), BF),
            pltpu.VMEM((3, 128, 128), F32),
            pltpu.VMEM((3072, 768), BF),
            pltpu.VMEM((768, 768), BF),
            pltpu.VMEM((2, 768, 768), BF),
            pltpu.VMEM((384, 768), BF),
            pltpu.VMEM((2, 6, 96, 768), BF),
            pltpu.VMEM((3, 96, 768), BF),
            pltpu.VMEM((2, 2, 96, 768), BF),
            pltpu.VMEM((2, 2, 192, 768), BF),
            pltpu.VMEM((2, 96, 768), BF),
            pltpu.VMEM((8, 896), F32),
            pltpu.VMEM((4, 8, 768), F32),
            pltpu.VMEM((4, 8, 896), F32),
            pltpu.VMEM((4, 8, 896), F32),
            pltpu.VMEM((2, 8, 128), F32),
            pltpu.VMEM((2, 768, 768), BF),
            pltpu.VMEM((2, 768, 768), BF),
            pltpu.SemaphoreType.DMA((4,)),
            pltpu.SemaphoreType.DMA((COPIES,)),
            pltpu.SemaphoreType.DMA((COPIES,)),
        ],
        compiler_params=pltpu.CompilerParams(
            collective_id=0, has_side_effects=True, vmem_limit_bytes=60 * 1024 * 1024
        ),
    )(
        embedded,
        expert_index[0],
        buckets,
        rel_bias,
        gain_attn,
        w_qkv[0],
        w_out[0],
        gain_ffn,
        w_router[0].astype(F32).T,
        w_in[0],
        w_down[0],
        cotangent,
    )
    rows = lambda size: pl.BlockSpec((size, 768), lambda i: (i, 0))
    whole = lambda *dims: pl.BlockSpec(dims, lambda i: (0,) * len(dims))
    shape = lambda *dims: jax.ShapeDtypeStruct(dims, F32)
    results = pl.pallas_call(
        widen,
        grid=(8,),
        in_specs=[
            rows(64),
            rows(64),
            rows(192),
            pl.BlockSpec((192, 768), lambda i: (i + 8, 0)),
            whole(768, 768),
            whole(8, 896),
        ],
        out_specs=[
            rows(64),
            rows(64),
            rows(192),
            rows(192),
            whole(3, 768, 192),
            whole(192, 768),
            whole(1, 768),
            whole(1, 768),
            whole(768, 2),
            whole(32, 3),
        ],
        out_shape=[
            shape(512, 768),
            shape(512, 768),
            shape(1536, 768),
            shape(1536, 768),
            shape(3, 768, 192),
            shape(192, 768),
            shape(1, 768),
            shape(1, 768),
            shape(768, 2),
            shape(32, 3),
        ],
        compiler_params=pltpu.CompilerParams(vmem_limit_bytes=40 * 1024 * 1024),
    )(hidden, grad_input, ffn, ffn, attn, small)
    hidden, grad_input, grad_in, grad_down, grad_qkv, grad_out = results[:6]
    grad_gain_attn, grad_gain_ffn, grad_router, grad_table = results[6:]
    return (
        hidden[None],
        grad_input[None],
        grad_table,
        grad_gain_attn,
        grad_qkv[None],
        grad_out[None],
        grad_gain_ffn,
        grad_router[None],
        grad_in.reshape(1, 2, 768, 768),
        grad_down.reshape(1, 2, 768, 768),
    )


def solution(mesh):
    in_specs = (
        P("dp", None),
        P("section", "dp", None),
        P(),
        P(None, "tensor"),
        P("section", None),
        P("section", None, None, "tensor"),
        P("section", "tensor", None),
        P("section", None),
        P("section", None, None),
        P("section", None, None, "tensor"),
        P("section", None, "tensor", None),
        P("dp", None),
    )
    out_specs = (
        P("section", "dp", None),
        P("section", "dp", None),
        P(None, "tensor"),
        P("section", None),
        P("section", None, None, "tensor"),
        P("section", "tensor", None),
        P("section", None),
        P("section", None, None),
        P("section", None, None, "tensor"),
        P("section", None, "tensor", None),
    )
    return jax.shard_map(shards, mesh=mesh, in_specs=in_specs, out_specs=out_specs, check_vma=False)
```

```python
import functools

import jax
import jax.numpy as jnp
from jax import lax
from jax.experimental import pallas as pl
from jax.experimental.pallas import tpu as pltpu
from jax.sharding import PartitionSpec as P

BF = jnp.bfloat16
F32 = jnp.float32
EPS = 1e-06
ROOT = 0.7978845608028654
CUBE = 0.044715
MB = 2
ROWS = 512 // MB
OWN = 128 // MB
HALF = OWN // 2
COPIES = 64 + 32 * MB


def dot(a, b):
    return jnp.dot(a, b, preferred_element_type=F32)


def dot_nt(a, b):
    return lax.dot_general(a, b, (((1,), (1,)), ((), ())), preferred_element_type=F32)


def dot_tn(a, b):
    return lax.dot_general(a, b, (((0,), (0,)), ((), ())), preferred_element_type=F32)


def wide(v):
    return v.astype(F32)


def inverse_rms(values):
    return lax.rsqrt(jnp.mean(values * values, axis=-1, keepdims=True) + EPS)


class Links:
    def __init__(self, send_sems, recv_sems):
        self.send_sems, self.recv_sems = send_sems, recv_sems
        self.used = 0
        self.pending = []

    def copy(self, src, dst, device, landing=None):
        return Copy(self, src, dst, device, landing)

    def drain(self):
        for out in self.pending:
            out.wait_send()
        self.pending = []


class Copy:
    def __init__(self, links, src, dst, device, landing):
        slot = links.used
        links.used += 1
        make = functools.partial(
            pltpu.make_async_remote_copy,
            src_ref=src,
            send_sem=links.send_sems.at[slot],
            recv_sem=links.recv_sems.at[slot],
            device_id=device,
            device_id_type=pl.DeviceIdType.MESH,
        )
        self.links = links
        self.out = make(dst_ref=dst)
        self.arriving = self.out if landing is None else make(dst_ref=landing)

    def start(self):
        self.out.start()
        self.links.pending.append(self.out)

    def wait(self):
        self.arriving.wait_recv()


class Gather:
    def __init__(self, links, at, right, left):
        copy = links.copy
        self.a_right = copy(at(0, 0), at(0, 0), right, at(3, 0))
        self.b_left = copy(at(0, 1), at(0, 1), left, at(1, 1))
        self.b_right = copy(at(0, 1), at(0, 1), right, at(3, 1))
        self.a_left = copy(at(0, 0), at(0, 0), left, at(1, 0))
        self.a_far = copy(at(3, 0), at(3, 0), right, at(2, 0))
        self.b_far = copy(at(1, 1), at(1, 1), left, at(2, 1))

    def start(self):
        for first in (self.a_right, self.b_left, self.b_right, self.a_left):
            first.start()

    def forward(self):
        self.a_right.wait()
        self.a_far.start()
        self.b_left.wait()
        self.b_far.start()

    def finish(self):
        for arriving in (self.b_right, self.a_left, self.a_far, self.b_far):
            arriving.wait()


class Scatter:
    def __init__(self, links, part, landed, summed, right, left):
        self.part, self.landed, self.summed = part, landed, summed
        copy = links.copy
        self.far_a = copy(part(2, 0), landed.at[0], right)
        self.far_b = copy(part(2, 1), landed.at[1], left)
        self.near_b = copy(part(1, 1), landed.at[2], right)
        self.near_a = copy(part(3, 0), landed.at[3], left)
        self.sum_a = copy(summed.at[0], landed.at[4], right)
        self.sum_b = copy(summed.at[1], landed.at[5], left)

    def start(self):
        for first in (self.far_a, self.far_b, self.near_b, self.near_a):
            first.start()

    def relay(self):
        part, landed, summed = self.part, self.landed, self.summed
        self.far_a.wait()
        summed[0] = (wide(landed[0]) + wide(part(1, 0)[...])).astype(BF)
        self.sum_a.start()
        self.far_b.wait()
        summed[1] = (wide(landed[1]) + wide(part(3, 1)[...])).astype(BF)
        self.sum_b.start()

    def finish(self):
        for arriving in (self.near_b, self.near_a, self.sum_a, self.sum_b):
            arriving.wait()
        landed, part = self.landed, self.part
        top = wide(part(0, 0)[...]) + wide(landed[3]) + wide(landed[4])
        bottom = wide(part(0, 1)[...]) + wide(landed[2]) + wide(landed[5])
        return jnp.concatenate([top, bottom], axis=0)


class DirectGather:
    def __init__(self, links, at, device):
        self.copies = [
            links.copy(at(0), at(0), device(k), at((4 - k) % 4)) for k in (2, 1, 3)
        ]

    def start(self):
        for out in self.copies:
            out.start()

    def forward(self):
        pass

    def finish(self):
        for arriving in self.copies:
            arriving.wait()


class DirectScatter:
    def __init__(self, links, part, landed, device):
        self.part, self.landed = part, landed
        self.copies = [
            links.copy(part(k), landed.at[i], device(k)) for i, k in enumerate((2, 1, 3))
        ]

    def start(self):
        for out in self.copies:
            out.start()

    def relay(self):
        pass

    def finish(self):
        for arriving in self.copies:
            arriving.wait()
        landed = self.landed
        return ((wide(self.part(0)[...]) + wide(landed[0])) + wide(landed[1])) + wide(landed[2])


class Reduce:
    def __init__(self, links, place, mates, grads, result, base, rows, pair, landed, summed, cross):
        (y, c), (ring, x_mate, c_mate) = place, mates
        self.grads, self.result, self.pair, self.cross = grads, result, pair, cross
        self.half, eighth, sixteenth = rows // 2, rows // 8, rows // 16
        self.mine = pl.multiple_of(base + c * self.half, 16)

        def at(ref):
            def view(k, half=None):
                start = self.mine + ((y + k) % 4) * eighth
                if half is None:
                    return ref.at[pl.ds(pl.multiple_of(start, 16), eighth)]
                start = start + half * sixteenth
                return ref.at[pl.ds(pl.multiple_of(start, 16), sixteenth)]

            return view

        theirs = pl.ds(pl.multiple_of(base + (1 - c) * self.half, 16), self.half)
        mine = pl.ds(self.mine, self.half)
        self.here = pl.ds(pl.multiple_of(self.mine + y * eighth, 16), eighth)
        self.paired = links.copy(grads.at[theirs], pair, c_mate)
        if summed is None:
            self.scatter = DirectScatter(links, at(grads), landed, ring)
        else:
            self.scatter = Scatter(links, at(grads), landed, summed, ring(1), ring(3))
        self.crossed = links.copy(cross.at[0], cross.at[1], x_mate)
        if summed is None:
            self.gather = DirectGather(links, at(result), ring)
        else:
            self.gather = Gather(links, at(result), ring(1), ring(3))
        self.shared = links.copy(result.at[mine], result.at[mine], c_mate, result.at[theirs])

    def pair_start(self):
        self.paired.start()

    def pair_finish(self):
        self.paired.wait()
        step = 96

        def add(i, carry):
            mine = pl.ds(pl.multiple_of(self.mine + i * step, 16), step)
            self.grads[mine, :] = (
                wide(self.grads[mine, :]) + wide(self.pair[pl.ds(i * step, step), :])
            ).astype(BF)
            return carry

        lax.fori_loop(0, self.half // step, add, 0)
        self.scatter.start()

    def relay(self):
        self.scatter.relay()

    def cross_start(self):
        self.cross[0] = self.scatter.finish().astype(BF)
        self.crossed.start()

    def cross_finish(self):
        self.crossed.wait()
        self.result[self.here, :] = (wide(self.cross[0]) + wide(self.cross[1])).astype(BF)
        self.gather.start()

    def forward(self):
        self.gather.forward()

    def share(self):
        self.gather.finish()
        self.shared.start()

    def finish(self):
        self.shared.wait()


def kernel(
    embedded,
    expert_index,
    buckets,
    rel_bias,
    gain_attn,
    w_qkv,
    w_out,
    gain_ffn,
    router,
    w_in_hbm,
    w_down_hbm,
    cotangent,
    out_hidden,
    out_input,
    out_ffn,
    out_attn,
    out_small,
    x_all,
    n_attn,
    heads,
    probs,
    bias,
    table_sums,
    att_all,
    w_out_all,
    middle,
    n_ffn,
    gate,
    expert,
    act,
    slope,
    part_a,
    part_b,
    part_c,
    landed_z,
    grad_top,
    grad_comb,
    grad_pre,
    grad_branch,
    grad_mid,
    grad_heads,
    grad_proj,
    table_rows,
    ffn_grads,
    attn_grads,
    ffn_pair,
    attn_pair,
    ffn_landed,
    attn_landed,
    ffn_summed,
    ffn_cross,
    attn_cross,
    small,
    small_z,
    small_y,
    small_xc,
    small_s,
    w_in,
    w_down,
    load_sems,
    send_sems,
    recv_sems,
):
    section, t, d = lax.axis_index("section"), lax.axis_index("tensor"), lax.axis_index("dp")
    y, xl, c = d // 4, (d // 2) % 2, d % 2
    ztx = lambda k: {"tensor": (t + k) % 4}
    ydx = lambda k: {"dp": (d + 4 * k) % 16}
    x_mate, c_mate = {"dp": d + 2 - 4 * xl}, {"dp": d + 1 - 2 * c}
    xc_mate = {"dp": d + 2 - 4 * xl + 1 - 2 * c}
    s_mate = {"section": 1 - section}
    links = Links(send_sems, recv_sems)

    load_in = pltpu.make_async_copy(w_in_hbm, w_in, load_sems.at[0])
    load_down = pltpu.make_async_copy(w_down_hbm, w_down, load_sems.at[1])
    load_embedded = pltpu.make_async_copy(embedded, x_all, load_sems.at[2])
    load_cotangent = pltpu.make_async_copy(cotangent, grad_top, load_sems.at[3])

    @pl.when(section == 0)
    def _():
        load_embedded.start()

    @pl.when(section == 1)
    def _():
        load_cotangent.start()

    load_in.start()
    load_down.start()
    barrier = pltpu.get_barrier_semaphore()
    mates = [ztx(1), ztx(2), ztx(3), ydx(1), ydx(2), ydx(3), x_mate, c_mate, xc_mate, s_mate]
    for mate in mates:
        pl.semaphore_signal(barrier, inc=1, device_id=mate, device_id_type=pl.DeviceIdType.MESH)

    def part_rows(m):
        return pl.ds(m * ROWS, ROWS)

    def own_rows(m):
        return pl.ds(pl.multiple_of(m * ROWS + t * OWN, OWN), OWN)

    def kept_rows(m):
        return pl.ds(m * OWN, OWN)

    def blocks(ref, m):
        return lambda k: ref.at[
            pl.ds(pl.multiple_of(m * ROWS + ((t + k) % 4) * OWN, OWN), OWN)
        ]

    def z_gather(at):
        return DirectGather(links, at, ztx)

    def z_scatter(part, kind, m):
        return DirectScatter(links, blocks(part, m), landed_z.at[kind, m], ztx)

    parts = range(MB)
    w_half = lambda k: w_out_all.at[(t + k) % 4, pl.ds(pl.multiple_of(c * 96, 16), 96)]
    w_rest = lambda k: w_out_all.at[(t + k) % 4, pl.ds(pl.multiple_of(96 - c * 96, 16), 96)]
    w_gather = z_gather(w_half)
    w_share = [links.copy(w_half(k), w_half(k), c_mate, w_rest(k)) for k in (1, 2, 3)]
    x_gather = [z_gather(blocks(x_all, m)) for m in parts]
    att_gather = [
        z_gather(lambda k, m=m: att_all.at[(t + k) % 4, pl.ds(m * ROWS, ROWS)])
        for m in parts
    ]
    ffn_scatter = [z_scatter(part_a, 0, m) for m in parts]
    hidden_gather = [z_gather(blocks(out_hidden, m)) for m in parts]
    top_gather = [z_gather(blocks(grad_top, m)) for m in parts]
    back_scatter = [z_scatter(part_b, 1, m) for m in parts]
    branch_gather = [z_gather(blocks(grad_branch, m)) for m in parts]
    attn_scatter = [z_scatter(part_c, 2, m) for m in parts]
    input_gather = [z_gather(blocks(out_input, m)) for m in parts]
    onward = [
        links.copy(out_hidden.at[own_rows(m)], x_all.at[own_rows(m)], s_mate) for m in parts
    ]
    returned = [
        links.copy(out_input.at[own_rows(m)], grad_top.at[own_rows(m)], s_mate) for m in parts
    ]
    place, ring = (y, c), (ydx, x_mate, c_mate)
    down_sum, in_sum = [
        Reduce(
            links,
            place,
            ring,
            ffn_grads,
            out_ffn,
            1536 * (1 - i),
            1536,
            ffn_pair.at[i],
            ffn_landed.at[i],
            ffn_summed.at[i],
            ffn_cross.at[i],
        )
        for i in range(2)
    ]
    attn_sum = Reduce(
        links,
        place,
        ring,
        attn_grads,
        out_attn,
        0,
        768,
        attn_pair,
        attn_landed,
        None,
        attn_cross,
    )
    small_over_z = [
        links.copy(small.at[:, 0:768], small_z.at[t], ztx(k), small_z.at[(t + 4 - k) % 4])
        for k in (1, 2, 3)
    ]
    small_over_y = [
        links.copy(small_y.at[y], small_y.at[y], ydx(k), small_y.at[(y + 4 - k) % 4])
        for k in (1, 2, 3)
    ]
    spot = 2 * xl + c
    small_over_xc = [
        links.copy(small_xc.at[spot], small_xc.at[spot], mate, small_xc.at[source])
        for mate, source in (
            (x_mate, 2 * (1 - xl) + c),
            (c_mate, 2 * xl + 1 - c),
            (xc_mate, 2 * (1 - xl) + 1 - c),
        )
    ]
    small_over_s = links.copy(small_s.at[0], small_s.at[1], s_mate)

    is_first = (expert_index[...] == 0).astype(F32)
    expert[...] = jnp.broadcast_to(is_first, (8, 512)).T[:, 0:1]
    w_out_all[t] = w_out[...]
    small[...] = jnp.zeros_like(small)
    table_sums[...] = jnp.zeros_like(table_sums)
    bias[...] = jnp.zeros_like(bias)
    table_rows[...] = jnp.zeros_like(table_rows)

    def add_bias(b, carry):
        hit = buckets[...] == b
        for h in range(3):
            bias[h] = jnp.where(hit, rel_bias[h, b], bias[h])
        return carry

    lax.fori_loop(0, 32, add_bias, 0)

    def router_gap():
        both = wide(router[...])
        return both[0:1, :] - both[1:2, :]

    def attention(m):
        rows = part_rows(m)
        values = wide(x_all[rows, :])
        normed = (values * inverse_rms(values) * gain_attn[...]).astype(BF)
        n_attn[rows, :] = normed
        projected = dot_nt(normed, w_qkv[...]).astype(BF)
        for i in range(9):
            heads[i, rows, :] = projected[:, i * 64 : (i + 1) * 64]
        for s in range(m * ROWS // 128, (m + 1) * ROWS // 128):
            rows = pl.ds(s * 128, 128)
            for h in range(3):
                scores = dot_nt(heads[h, rows, :], heads[3 + h, rows, :]) * 0.125 + bias[h]
                powers = jnp.exp(scores - jnp.max(scores, axis=-1, keepdims=True))
                weights = powers / jnp.sum(powers, axis=-1, keepdims=True)
                probs[3 * s + h] = weights
                att_all[t, rows, h * 64 : (h + 1) * 64] = dot(
                    weights.astype(BF), heads[6 + h, rows, :]
                ).astype(BF)
        att_gather[m].start()

    def experts(m):
        rows = part_rows(m)
        att_gather[m].finish()
        total = wide(x_all[rows, :])
        for source in range(4):
            total = total + dot(att_all[source, rows, :], w_out_all[source])
        middle[rows, :] = total
        normed = (total * inverse_rms(total) * gain_ffn[...]).astype(BF)
        n_ffn[rows, :] = normed
        chosen = expert[rows, :]
        gap = jnp.sum(wide(normed) * router_gap(), axis=-1, keepdims=True)
        gate[rows, :] = 1.0 / (1.0 + jnp.exp(jnp.where(chosen > 0.5, -gap, gap)))
        pre = jnp.where(chosen > 0.5, dot(normed, w_in[0]), dot(normed, w_in[1]))
        square = pre * pre
        bent = jnp.tanh(ROOT * pre * (1.0 + CUBE * square))
        active = 0.5 * pre * (1.0 + bent)
        slope[rows, :] = 0.5 * (1.0 + bent) + (0.5 * ROOT) * pre * (1.0 - bent * bent) * (
            1.0 + 3.0 * CUBE * square
        )
        active_low = active.astype(BF)
        act[rows, :] = active_low
        down = jnp.where(chosen > 0.5, dot(active_low, w_down[0]), dot(active_low, w_down[1]))
        part_a[rows, :] = down.astype(BF)

    def end_layer(m):
        combined = ffn_scatter[m].finish()
        own = own_rows(m)
        out_hidden[own, :] = (middle[own, :] + gate[own, :] * combined).astype(BF)

    def experts_back(m):
        rows = part_rows(m)
        chosen, share = expert[rows, :], gate[rows, :]
        top = wide(grad_top[rows, :])
        low = (share * top).astype(BF)
        grad_comb[rows, :] = low
        into = jnp.where(chosen > 0.5, dot_nt(low, w_down[0]), dot_nt(low, w_down[1]))
        pre_low = (into * slope[rows, :]).astype(BF)
        grad_pre[rows, :] = pre_low
        back = jnp.where(chosen > 0.5, dot_nt(pre_low, w_in[0]), dot_nt(pre_low, w_in[1]))
        grad_gate = jnp.sum(top * wide(part_a[rows, :]), axis=-1, keepdims=True)
        logit = share * (1.0 - share) * grad_gate * (2.0 * chosen - 1.0)
        small[0:1, 0:768] += jnp.sum(wide(n_ffn[rows, :]) * logit, axis=0, keepdims=True)
        part_b[rows, :] = (back + logit * router_gap()).astype(BF)
        back_scatter[m].start()

    def w_spread():
        w_gather.finish()
        for out in w_share:
            out.start()

    def w_finish():
        for arriving in w_share:
            arriving.wait()

    def middle_back(m):
        own = own_rows(m)
        grad_nffn = back_scatter[m].finish()
        values = middle[own, :]
        scale = inverse_rms(values)
        small[3:4, 0:768] += jnp.sum(grad_nffn * values * scale, axis=0, keepdims=True)
        g = grad_nffn * gain_ffn[...]
        inner = jnp.mean(g * values, axis=-1, keepdims=True)
        grad_middle = wide(grad_top[own, :]) + scale * (g - values * scale * scale * inner)
        grad_mid[kept_rows(m), :] = grad_middle
        grad_branch[own, :] = grad_middle.astype(BF)
        branch_gather[m].start()

    def attention_back(m):
        rows = part_rows(m)
        branch_gather[m].finish()
        grad_att = dot_nt(grad_branch[rows, :], w_out[...]).astype(BF)
        for h in range(3):
            grad_heads[h, rows, :] = grad_att[:, h * 64 : (h + 1) * 64]
        for s in range(m * ROWS // 128, (m + 1) * ROWS // 128):
            rows = pl.ds(s * 128, 128)
            for h in range(3):
                weights = probs[3 * s + h]
                grad_att = grad_heads[h, rows, :]
                grad_w = dot_nt(grad_att, heads[6 + h, rows, :])
                mean = jnp.sum(weights * grad_w, axis=-1, keepdims=True)
                low = (weights * (grad_w - mean)).astype(BF)
                table_sums[h] += wide(low)
                at = h * 64
                grad_proj[rows, at : at + 64] = (0.125 * dot(low, heads[3 + h, rows, :])).astype(BF)
                at = 192 + h * 64
                grad_proj[rows, at : at + 64] = (0.125 * dot_tn(low, heads[h, rows, :])).astype(BF)
                at = 384 + h * 64
                grad_proj[rows, at : at + 64] = dot_tn(weights.astype(BF), grad_att).astype(BF)
        rows = part_rows(m)
        part_c[rows, :] = dot(grad_proj[rows, :], w_qkv[...]).astype(BF)
        attn_scatter[m].start()

    def input_back(m):
        own = own_rows(m)
        grad_nattn = attn_scatter[m].finish()
        values = wide(x_all[own, :])
        scale = inverse_rms(values)
        small[2:3, 0:768] += jnp.sum(grad_nattn * values * scale, axis=0, keepdims=True)
        q = grad_nattn * gain_attn[...]
        inner = jnp.mean(q * values, axis=-1, keepdims=True)
        out_input[own, :] = (
            grad_mid[kept_rows(m), :] + scale * (q - values * scale * scale * inner)
        ).astype(BF)

    def expert_grads(base, left, right):
        for e in range(2):
            mask = expert[...] if e == 0 else 1.0 - expert[...]
            masked = right[...] * mask.astype(BF)
            ffn_grads[pl.ds(base + e * 768, 768), :] = dot_tn(left[...], masked).astype(BF)

    def down_grads():
        expert_grads(1536, act, grad_comb)
        down_sum.pair_start()

    def in_grads():
        expert_grads(0, n_ffn, grad_pre)
        in_sum.pair_start()

    def attention_grads():
        attn_grads[0:576, :] = dot_tn(grad_proj[...], n_attn[...]).astype(BF)
        attn_grads[576:768, :] = dot_tn(att_all[t], grad_branch[...]).astype(BF)
        attn_sum.pair_start()

    def small_z_start():
        small[1:2, 0:768] = -small[0:1, 0:768]
        small_z[t] = small[:, 0:768]
        for out in small_over_z:
            out.start()

    def table():
        def add_table(b, carry):
            hit = buckets[...] == b
            for h in range(3):
                table_rows[h, pl.ds(b, 1), :] = jnp.sum(
                    jnp.where(hit, table_sums[h], 0.0), axis=0, keepdims=True
                )
            return carry

        lax.fori_loop(0, 32, add_table, 0)
        for h in range(3):
            line = lax.dot_general(
                jnp.ones((8, 128), F32),
                table_rows[h],
                (((1,), (1,)), ((), ())),
                precision=lax.Precision.HIGHEST,
                preferred_element_type=F32,
            )
            small[h : h + 1, 768:896] = line[0:1, :]

    def small_y_start():
        for arriving in small_over_z:
            arriving.wait()
        small_y[y, :, 0:768] = ((small_z[0] + small_z[1]) + small_z[2]) + small_z[3]
        small_y[y, :, 768:896] = small[:, 768:896]
        for out in small_over_y:
            out.start()

    def small_xc_start():
        for arriving in small_over_y:
            arriving.wait()
        small_xc[spot] = ((small_y[0] + small_y[1]) + small_y[2]) + small_y[3]
        for out in small_over_xc:
            out.start()

    def small_s_start():
        for arriving in small_over_xc:
            arriving.wait()
        total = ((small_xc[0] + small_xc[1]) + small_xc[2]) + small_xc[3]
        out_small[...] = total
        small_s[0] = total[:, 768:896]
        small_over_s.start()

    def small_end():
        small_over_s.wait()
        out_small[:, 768:896] = small_s[0] + small_s[1]

    pl.semaphore_wait(barrier, len(mates))
    w_gather.start()
    opening = links.pending

    @pl.when(section == 0)
    def _():
        links.pending = list(opening)

        def middle_up(m):
            experts(m)
            ffn_scatter[m].start()

        def pass_on(m):
            end_layer(m)
            onward[m].start()
            hidden_gather[m].start()

        load_embedded.wait()
        attention(0)
        w_spread()
        attention(1)
        load_in.wait()
        load_down.wait()
        w_finish()
        middle_up(0)
        middle_up(1)
        pass_on(0)
        pass_on(1)
        for m in parts:
            returned[m].wait()
            top_gather[m].start()
        for m in parts:
            top_gather[m].finish()
            experts_back(m)
        down_grads()
        in_grads()
        down_sum.pair_finish()
        in_sum.pair_finish()
        middle_back(0)
        middle_back(1)
        down_sum.relay()
        attention_back(0)
        in_sum.relay()
        attention_back(1)
        attention_grads()
        down_sum.cross_start()
        input_back(0)
        input_gather[0].start()
        attn_sum.pair_finish()
        input_back(1)
        input_gather[1].start()
        in_sum.cross_start()
        small_z_start()
        table()
        down_sum.cross_finish()
        small_y_start()
        attn_sum.cross_start()
        in_sum.cross_finish()
        down_sum.forward()
        small_xc_start()
        attn_sum.cross_finish()
        in_sum.forward()
        small_s_start()
        down_sum.share()
        in_sum.share()
        attn_sum.share()
        small_end()
        for unit in (down_sum, in_sum, attn_sum):
            unit.finish()
        for m in parts:
            hidden_gather[m].finish()
            input_gather[m].finish()
        links.drain()

    @pl.when(section == 1)
    def _():
        links.pending = list(opening)
        load_cotangent.wait()
        load_in.wait()
        load_down.wait()
        w_spread()
        w_finish()
        for m in parts:
            onward[m].wait()
            x_gather[m].start()
        for m in parts:
            x_gather[m].finish()
            attention(m)
        for m in parts:
            experts(m)
            experts_back(m)
        for m in parts:
            middle_back(m)
        for m in parts:
            attention_back(m)
        for m in parts:
            input_back(m)
            returned[m].start()
        for m in parts:
            input_gather[m].start()
            ffn_scatter[m].start()
        down_grads()
        in_grads()
        attention_grads()
        down_sum.pair_finish()
        in_sum.pair_finish()
        attn_sum.pair_finish()
        small_z_start()
        table()
        for m in parts:
            end_layer(m)
            hidden_gather[m].start()
        small_y_start()
        small_xc_start()
        small_s_start()
        for step in ("relay", "cross_start", "cross_finish", "forward", "share", "finish"):
            for unit in (down_sum, in_sum, attn_sum):
                getattr(unit, step)()
        for m in parts:
            hidden_gather[m].finish()
            input_gather[m].finish()
        small_end()
        links.drain()


def widen(hidden, grad_input, ffn_in, ffn_down, attn_qkv, attn_out, small, *outs):
    for low, out in zip((hidden, grad_input, ffn_in, ffn_down, attn_qkv, attn_out), outs):
        out[...] = wide(low[...])
    out_router, out_gain_attn, out_gain_ffn, out_table = outs[6:]

    @pl.when(pl.program_id(0) == 0)
    def _():
        out_router[...] = small[0:2, 0:768]
        out_gain_attn[...] = small[2:3, 0:768]
        out_gain_ffn[...] = small[3:4, 0:768]
        out_table[...] = small[0:3, 768:800]


def shards(
    embedded,
    expert_index,
    buckets,
    rel_bias,
    gain_attn,
    w_qkv,
    w_out,
    gain_ffn,
    w_router,
    w_in,
    w_down,
    cotangent,
):
    vmem, smem = pl.BlockSpec(memory_space=pltpu.VMEM), pl.BlockSpec(memory_space=pltpu.SMEM)
    anywhere = pl.BlockSpec(memory_space=pl.ANY)
    hidden, grad_input, ffn, attn, small = pl.pallas_call(
        kernel,
        out_shape=[
            jax.ShapeDtypeStruct((512, 768), BF),
            jax.ShapeDtypeStruct((512, 768), BF),
            jax.ShapeDtypeStruct((3072, 768), BF),
            jax.ShapeDtypeStruct((768, 768), BF),
            jax.ShapeDtypeStruct((8, 896), F32),
        ],
        in_specs=[anywhere, vmem, vmem, smem] + [vmem] * 5 + [anywhere] * 3,
        out_specs=[vmem] * 5,
        scratch_shapes=[
            pltpu.VMEM((512, 768), BF),
            pltpu.VMEM((512, 768), BF),
            pltpu.VMEM((9, 512, 64), BF),
            pltpu.VMEM((12, 128, 128), F32),
            pltpu.VMEM((3, 128, 128), F32),
            pltpu.VMEM((3, 128, 128), F32),
            pltpu.VMEM((4, 512, 192), BF),
            pltpu.VMEM((4, 192, 768), BF),
            pltpu.VMEM((512, 768), F32),
            pltpu.VMEM((512, 768), BF),
            pltpu.VMEM((512, 1), F32),
            pltpu.VMEM((512, 1), F32),
            pltpu.VMEM((512, 768), BF),
            pltpu.VMEM((512, 768), F32),
            pltpu.VMEM((512, 768), BF),
            pltpu.VMEM((512, 768), BF),
            pltpu.VMEM((512, 768), BF),
            pltpu.VMEM((3, MB, 3, OWN, 768), BF),
            pltpu.VMEM((512, 768), BF),
            pltpu.VMEM((512, 768), BF),
            pltpu.VMEM((512, 768), BF),
            pltpu.VMEM((512, 768), BF),
            pltpu.VMEM((128, 768), F32),
            pltpu.VMEM((3, 512, 64), BF),
            pltpu.VMEM((512, 576), BF),
            pltpu.VMEM((3, 128, 128), F32),
            pltpu.VMEM((3072, 768), BF),
            pltpu.VMEM((768, 768), BF),
            pltpu.VMEM((2, 768, 768), BF),
            pltpu.VMEM((384, 768), BF),
            pltpu.VMEM((2, 6, 96, 768), BF),
            pltpu.VMEM((3, 96, 768), BF),
            pltpu.VMEM((2, 2, 96, 768), BF),
            pltpu.VMEM((2, 2, 192, 768), BF),
            pltpu.VMEM((2, 96, 768), BF),
            pltpu.VMEM((8, 896), F32),
            pltpu.VMEM((4, 8, 768), F32),
            pltpu.VMEM((4, 8, 896), F32),
            pltpu.VMEM((4, 8, 896), F32),
            pltpu.VMEM((2, 8, 128), F32),
            pltpu.VMEM((2, 768, 768), BF),
            pltpu.VMEM((2, 768, 768), BF),
            pltpu.SemaphoreType.DMA((4,)),
            pltpu.SemaphoreType.DMA((COPIES,)),
            pltpu.SemaphoreType.DMA((COPIES,)),
        ],
        compiler_params=pltpu.CompilerParams(
            collective_id=0, has_side_effects=True, vmem_limit_bytes=60 * 1024 * 1024
        ),
    )(
        embedded,
        expert_index.reshape(1, 512),
        buckets,
        rel_bias.T,
        gain_attn,
        jnp.transpose(w_qkv[0], (0, 2, 1)).reshape(576, 768),
        w_out[0],
        gain_ffn,
        w_router[0].T,
        w_in[0],
        w_down[0],
        cotangent,
    )
    rows = lambda size, start=0: pl.BlockSpec((size, 768), lambda i: (i + start, 0))
    whole = lambda *dims: pl.BlockSpec(dims, lambda i: (0,) * len(dims))
    shape = lambda *dims: jax.ShapeDtypeStruct(dims, F32)
    results = pl.pallas_call(
        widen,
        grid=(4,),
        in_specs=[
            rows(128),
            rows(128),
            rows(384),
            rows(384, 4),
            rows(144),
            rows(48, 12),
            whole(8, 896),
        ],
        out_specs=[
            rows(128),
            rows(128),
            rows(384),
            rows(384),
            rows(144),
            rows(48),
            whole(2, 768),
            whole(1, 768),
            whole(1, 768),
            whole(3, 32),
        ],
        out_shape=[
            shape(512, 768),
            shape(512, 768),
            shape(1536, 768),
            shape(1536, 768),
            shape(576, 768),
            shape(192, 768),
            shape(2, 768),
            shape(1, 768),
            shape(1, 768),
            shape(3, 32),
        ],
        compiler_params=pltpu.CompilerParams(vmem_limit_bytes=60 * 1024 * 1024),
    )(hidden, grad_input, ffn, ffn, attn, attn, small)
    hidden, grad_input, grad_in, grad_down, grad_qkv, grad_out = results[:6]
    grad_router, grad_gain_attn, grad_gain_ffn, grad_table = results[6:]
    return (
        hidden[None],
        grad_input[None],
        grad_table.T,
        grad_gain_attn,
        jnp.transpose(grad_qkv.reshape(1, 3, 192, 768), (0, 1, 3, 2)),
        grad_out[None],
        grad_gain_ffn,
        grad_router.T[None],
        grad_in.reshape(1, 2, 768, 768),
        grad_down.reshape(1, 2, 768, 768),
    )


def solution(mesh):
    in_specs = (
        P("dp", None),
        P("section", "dp", None),
        P(),
        P(None, "tensor"),
        P("section", None),
        P("section", None, None, "tensor"),
        P("section", "tensor", None),
        P("section", None),
        P("section", None, None),
        P("section", None, None, "tensor"),
        P("section", None, "tensor", None),
        P("dp", None),
    )
    out_specs = (
        P("section", "dp", None),
        P("section", "dp", None),
        P(None, "tensor"),
        P("section", None),
        P("section", None, None, "tensor"),
        P("section", "tensor", None),
        P("section", None),
        P("section", None, None),
        P("section", None, None, "tensor"),
        P("section", None, "tensor", None),
    )
    return jax.shard_map(shards, mesh=mesh, in_specs=in_specs, out_specs=out_specs, check_vma=False)
```

```python
import functools

import jax
import jax.numpy as jnp
from jax import lax
from jax.experimental import pallas as pl
from jax.experimental.pallas import tpu as pltpu
from jax.sharding import PartitionSpec as P

BF = jnp.bfloat16
F32 = jnp.float32
EPS = 1e-06
ROOT = 0.7978845608028654
CUBE = 0.044715
MB = 2
ROWS = 512 // MB
OWN = 128 // MB
HALF = OWN // 2
COPIES = 64 + 32 * MB


def dot(a, b):
    return jnp.dot(a, b, preferred_element_type=F32)


def dot_nt(a, b):
    return lax.dot_general(a, b, (((1,), (1,)), ((), ())), preferred_element_type=F32)


def dot_tn(a, b):
    return lax.dot_general(a, b, (((0,), (0,)), ((), ())), preferred_element_type=F32)


def wide(v):
    return v.astype(F32)


def inverse_rms(values):
    return lax.rsqrt(jnp.mean(values * values, axis=-1, keepdims=True) + EPS)


class Links:
    def __init__(self, send_sems, recv_sems):
        self.send_sems, self.recv_sems = send_sems, recv_sems
        self.used = 0
        self.pending = []

    def copy(self, src, dst, device, landing=None):
        return Copy(self, src, dst, device, landing)

    def drain(self):
        for out in self.pending:
            out.wait_send()
        self.pending = []


class Copy:
    def __init__(self, links, src, dst, device, landing):
        slot = links.used
        links.used += 1
        make = functools.partial(
            pltpu.make_async_remote_copy,
            src_ref=src,
            send_sem=links.send_sems.at[slot],
            recv_sem=links.recv_sems.at[slot],
            device_id=device,
            device_id_type=pl.DeviceIdType.MESH,
        )
        self.links = links
        self.out = make(dst_ref=dst)
        self.arriving = self.out if landing is None else make(dst_ref=landing)

    def start(self):
        self.out.start()
        self.links.pending.append(self.out)

    def wait(self):
        self.arriving.wait_recv()


class Gather:
    def __init__(self, links, at, right, left):
        copy = links.copy
        self.a_right = copy(at(0, 0), at(0, 0), right, at(3, 0))
        self.b_left = copy(at(0, 1), at(0, 1), left, at(1, 1))
        self.b_right = copy(at(0, 1), at(0, 1), right, at(3, 1))
        self.a_left = copy(at(0, 0), at(0, 0), left, at(1, 0))
        self.a_far = copy(at(3, 0), at(3, 0), right, at(2, 0))
        self.b_far = copy(at(1, 1), at(1, 1), left, at(2, 1))

    def start(self):
        for first in (self.a_right, self.b_left, self.b_right, self.a_left):
            first.start()

    def forward(self):
        self.a_right.wait()
        self.a_far.start()
        self.b_left.wait()
        self.b_far.start()

    def finish(self):
        for arriving in (self.b_right, self.a_left, self.a_far, self.b_far):
            arriving.wait()


class Scatter:
    def __init__(self, links, part, landed, summed, right, left):
        self.part, self.landed, self.summed = part, landed, summed
        copy = links.copy
        self.far_a = copy(part(2, 0), landed.at[0], right)
        self.far_b = copy(part(2, 1), landed.at[1], left)
        self.near_b = copy(part(1, 1), landed.at[2], right)
        self.near_a = copy(part(3, 0), landed.at[3], left)
        self.sum_a = copy(summed.at[0], landed.at[4], right)
        self.sum_b = copy(summed.at[1], landed.at[5], left)

    def start(self):
        for first in (self.far_a, self.far_b, self.near_b, self.near_a):
            first.start()

    def relay(self):
        part, landed, summed = self.part, self.landed, self.summed
        self.far_a.wait()
        summed[0] = (wide(landed[0]) + wide(part(1, 0)[...])).astype(BF)
        self.sum_a.start()
        self.far_b.wait()
        summed[1] = (wide(landed[1]) + wide(part(3, 1)[...])).astype(BF)
        self.sum_b.start()

    def finish(self):
        for arriving in (self.near_b, self.near_a, self.sum_a, self.sum_b):
            arriving.wait()
        landed, part = self.landed, self.part
        top = wide(part(0, 0)[...]) + wide(landed[3]) + wide(landed[4])
        bottom = wide(part(0, 1)[...]) + wide(landed[2]) + wide(landed[5])
        return jnp.concatenate([top, bottom], axis=0)


class DirectGather:
    def __init__(self, links, at, device):
        self.copies = [
            links.copy(at(0), at(0), device(k), at((4 - k) % 4)) for k in (2, 1, 3)
        ]

    def start(self):
        for out in self.copies:
            out.start()

    def forward(self):
        pass

    def finish(self):
        for arriving in self.copies:
            arriving.wait()


class DirectScatter:
    def __init__(self, links, part, landed, device):
        self.part, self.landed = part, landed
        self.copies = [
            links.copy(part(k), landed.at[i], device(k)) for i, k in enumerate((2, 1, 3))
        ]

    def start(self):
        for out in self.copies:
            out.start()

    def relay(self):
        pass

    def finish(self):
        for arriving in self.copies:
            arriving.wait()
        landed = self.landed
        return ((wide(self.part(0)[...]) + wide(landed[0])) + wide(landed[1])) + wide(landed[2])


class Reduce:
    def __init__(self, links, place, mates, grads, result, base, rows, pair, landed, summed, cross):
        (y, c), (ring, x_mate, c_mate) = place, mates
        self.grads, self.result, self.pair, self.cross = grads, result, pair, cross
        self.half, eighth, sixteenth = rows // 2, rows // 8, rows // 16
        self.mine = pl.multiple_of(base + c * self.half, 16)

        def at(ref):
            def view(k, half=None):
                start = self.mine + ((y + k) % 4) * eighth
                if half is None:
                    return ref.at[pl.ds(pl.multiple_of(start, 16), eighth)]
                start = start + half * sixteenth
                return ref.at[pl.ds(pl.multiple_of(start, 16), sixteenth)]

            return view

        theirs = pl.ds(pl.multiple_of(base + (1 - c) * self.half, 16), self.half)
        mine = pl.ds(self.mine, self.half)
        self.here = pl.ds(pl.multiple_of(self.mine + y * eighth, 16), eighth)
        self.paired = links.copy(grads.at[theirs], pair, c_mate)
        if summed is None:
            self.scatter = DirectScatter(links, at(grads), landed, ring)
        else:
            self.scatter = Scatter(links, at(grads), landed, summed, ring(1), ring(3))
        self.crossed = links.copy(cross.at[0], cross.at[1], x_mate)
        if summed is None:
            self.gather = DirectGather(links, at(result), ring)
        else:
            self.gather = Gather(links, at(result), ring(1), ring(3))
        self.shared = links.copy(result.at[mine], result.at[mine], c_mate, result.at[theirs])

    def pair_start(self):
        self.paired.start()

    def pair_finish(self):
        self.paired.wait()
        step = 96

        def add(i, carry):
            mine = pl.ds(pl.multiple_of(self.mine + i * step, 16), step)
            self.grads[mine, :] = (
                wide(self.grads[mine, :]) + wide(self.pair[pl.ds(i * step, step), :])
            ).astype(BF)
            return carry

        lax.fori_loop(0, self.half // step, add, 0)
        self.scatter.start()

    def relay(self):
        self.scatter.relay()

    def cross_start(self):
        self.cross[0] = self.scatter.finish().astype(BF)
        self.crossed.start()

    def cross_finish(self):
        self.crossed.wait()
        self.result[self.here, :] = (wide(self.cross[0]) + wide(self.cross[1])).astype(BF)
        self.gather.start()

    def forward(self):
        self.gather.forward()

    def share(self):
        self.gather.finish()
        self.shared.start()

    def finish(self):
        self.shared.wait()


def kernel(
    embedded,
    expert_index,
    buckets,
    rel_bias,
    gain_attn,
    w_qkv,
    w_out,
    gain_ffn,
    router,
    w_in_hbm,
    w_down_hbm,
    cotangent,
    hidden_hbm,
    input_hbm,
    ffn_hbm,
    attn_hbm,
    out_small,
    out_hidden,
    out_input,
    out_ffn,
    out_attn,
    x_all,
    n_attn,
    heads,
    probs,
    bias,
    table_sums,
    att_all,
    w_out_all,
    middle,
    n_ffn,
    gate,
    expert,
    act,
    slope,
    part_a,
    part_b,
    part_c,
    landed_z,
    grad_top,
    grad_comb,
    grad_pre,
    grad_branch,
    grad_mid,
    grad_heads,
    grad_proj,
    table_rows,
    ffn_grads,
    attn_grads,
    ffn_pair,
    attn_pair,
    ffn_landed,
    attn_landed,
    ffn_summed,
    ffn_cross,
    attn_cross,
    small,
    small_z,
    small_y,
    small_xc,
    small_s,
    w_in,
    w_down,
    load_sems,
    send_sems,
    recv_sems,
):
    section, t, d = lax.axis_index("section"), lax.axis_index("tensor"), lax.axis_index("dp")
    y, xl, c = d // 4, (d // 2) % 2, d % 2
    ztx = lambda k: {"tensor": (t + k) % 4}
    ydx = lambda k: {"dp": (d + 4 * k) % 16}
    x_mate, c_mate = {"dp": d + 2 - 4 * xl}, {"dp": d + 1 - 2 * c}
    xc_mate = {"dp": d + 2 - 4 * xl + 1 - 2 * c}
    s_mate = {"section": 1 - section}
    links = Links(send_sems, recv_sems)

    keep_hidden = pltpu.make_async_copy(out_hidden, hidden_hbm, load_sems.at[4])
    keep_input = pltpu.make_async_copy(out_input, input_hbm, load_sems.at[5])
    keep_in, keep_down = [
        pltpu.make_async_copy(
            out_ffn.at[pl.ds(i * 1536, 1536)], ffn_hbm.at[pl.ds(i * 1536, 1536)], load_sems.at[6 + i]
        )
        for i in range(2)
    ]
    keep_attn = pltpu.make_async_copy(out_attn, attn_hbm, load_sems.at[8])
    load_in = pltpu.make_async_copy(w_in_hbm, w_in, load_sems.at[0])
    load_down = pltpu.make_async_copy(w_down_hbm, w_down, load_sems.at[1])
    load_embedded = pltpu.make_async_copy(embedded, x_all, load_sems.at[2])
    load_cotangent = pltpu.make_async_copy(cotangent, grad_top, load_sems.at[3])

    @pl.when(section == 0)
    def _():
        load_embedded.start()

    @pl.when(section == 1)
    def _():
        load_cotangent.start()

    load_in.start()
    load_down.start()
    barrier = pltpu.get_barrier_semaphore()
    mates = [ztx(1), ztx(2), ztx(3), ydx(1), ydx(2), ydx(3), x_mate, c_mate, xc_mate, s_mate]
    for mate in mates:
        pl.semaphore_signal(barrier, inc=1, device_id=mate, device_id_type=pl.DeviceIdType.MESH)

    def part_rows(m):
        return pl.ds(m * ROWS, ROWS)

    def own_rows(m):
        return pl.ds(pl.multiple_of(m * ROWS + t * OWN, OWN), OWN)

    def kept_rows(m):
        return pl.ds(m * OWN, OWN)

    def blocks(ref, m):
        return lambda k: ref.at[
            pl.ds(pl.multiple_of(m * ROWS + ((t + k) % 4) * OWN, OWN), OWN)
        ]

    def z_gather(at):
        return DirectGather(links, at, ztx)

    def z_scatter(part, kind, m):
        return DirectScatter(links, blocks(part, m), landed_z.at[kind, m], ztx)

    parts = range(MB)
    w_half = lambda k: w_out_all.at[(t + k) % 4, pl.ds(pl.multiple_of(c * 96, 16), 96)]
    w_rest = lambda k: w_out_all.at[(t + k) % 4, pl.ds(pl.multiple_of(96 - c * 96, 16), 96)]
    w_gather = z_gather(w_half)
    w_share = [links.copy(w_half(k), w_half(k), c_mate, w_rest(k)) for k in (1, 2, 3)]
    x_gather = [z_gather(blocks(x_all, m)) for m in parts]
    att_gather = [
        z_gather(lambda k, m=m: att_all.at[(t + k) % 4, pl.ds(m * ROWS, ROWS)])
        for m in parts
    ]
    ffn_scatter = [z_scatter(part_a, 0, m) for m in parts]
    hidden_gather = [z_gather(blocks(out_hidden, m)) for m in parts]
    top_gather = [z_gather(blocks(grad_top, m)) for m in parts]
    back_scatter = [z_scatter(part_b, 1, m) for m in parts]
    branch_gather = [z_gather(blocks(grad_branch, m)) for m in parts]
    attn_scatter = [z_scatter(part_c, 2, m) for m in parts]
    input_gather = [z_gather(blocks(out_input, m)) for m in parts]
    onward = [
        links.copy(out_hidden.at[own_rows(m)], x_all.at[own_rows(m)], s_mate) for m in parts
    ]
    returned = [
        links.copy(out_input.at[own_rows(m)], grad_top.at[own_rows(m)], s_mate) for m in parts
    ]
    place, ring = (y, c), (ydx, x_mate, c_mate)
    down_sum, in_sum = [
        Reduce(
            links,
            place,
            ring,
            ffn_grads,
            out_ffn,
            1536 * (1 - i),
            1536,
            ffn_pair.at[i],
            ffn_landed.at[i],
            ffn_summed.at[i],
            ffn_cross.at[i],
        )
        for i in range(2)
    ]
    attn_sum = Reduce(
        links,
        place,
        ring,
        attn_grads,
        out_attn,
        0,
        768,
        attn_pair,
        attn_landed,
        None,
        attn_cross,
    )
    small_over_z = [
        links.copy(small.at[:, 0:768], small_z.at[t], ztx(k), small_z.at[(t + 4 - k) % 4])
        for k in (1, 2, 3)
    ]
    small_over_y = [
        links.copy(small_y.at[y], small_y.at[y], ydx(k), small_y.at[(y + 4 - k) % 4])
        for k in (1, 2, 3)
    ]
    spot = 2 * xl + c
    small_over_xc = [
        links.copy(small_xc.at[spot], small_xc.at[spot], mate, small_xc.at[source])
        for mate, source in (
            (x_mate, 2 * (1 - xl) + c),
            (c_mate, 2 * xl + 1 - c),
            (xc_mate, 2 * (1 - xl) + 1 - c),
        )
    ]
    small_over_s = links.copy(small_s.at[0], small_s.at[1], s_mate)

    is_first = (expert_index[...] == 0).astype(F32)
    expert[...] = jnp.broadcast_to(is_first, (8, 512)).T[:, 0:1]
    w_out_all[t] = w_out[...]
    small[...] = jnp.zeros_like(small)
    table_sums[...] = jnp.zeros_like(table_sums)
    bias[...] = jnp.zeros_like(bias)
    table_rows[...] = jnp.zeros_like(table_rows)

    def add_bias(b, carry):
        hit = buckets[...] == b
        for h in range(3):
            bias[h] = jnp.where(hit, rel_bias[h, b], bias[h])
        return carry

    lax.fori_loop(0, 32, add_bias, 0)

    def router_gap():
        both = wide(router[...])
        return both[0:1, :] - both[1:2, :]

    def attention(m):
        rows = part_rows(m)
        values = wide(x_all[rows, :])
        normed = (values * inverse_rms(values) * gain_attn[...]).astype(BF)
        n_attn[rows, :] = normed
        projected = dot_nt(normed, w_qkv[...]).astype(BF)
        for i in range(9):
            heads[i, rows, :] = projected[:, i * 64 : (i + 1) * 64]
        for s in range(m * ROWS // 128, (m + 1) * ROWS // 128):
            rows = pl.ds(s * 128, 128)
            for h in range(3):
                scores = dot_nt(heads[h, rows, :], heads[3 + h, rows, :]) * 0.125 + bias[h]
                powers = jnp.exp(scores - jnp.max(scores, axis=-1, keepdims=True))
                weights = powers * (1.0 / jnp.sum(powers, axis=-1, keepdims=True))
                probs[3 * s + h] = weights
                att_all[t, rows, h * 64 : (h + 1) * 64] = dot(
                    weights.astype(BF), heads[6 + h, rows, :]
                ).astype(BF)
        att_gather[m].start()

    def experts(m):
        rows = part_rows(m)
        att_gather[m].finish()
        total = wide(x_all[rows, :])
        for source in range(4):
            total = total + dot(att_all[source, rows, :], w_out_all[source])
        middle[rows, :] = total
        normed = (total * inverse_rms(total) * gain_ffn[...]).astype(BF)
        n_ffn[rows, :] = normed
        chosen = expert[rows, :]
        gap = jnp.sum(wide(normed) * router_gap(), axis=-1, keepdims=True)
        gate[rows, :] = 1.0 / (1.0 + jnp.exp(jnp.where(chosen > 0.5, -gap, gap)))
        pre = jnp.where(chosen > 0.5, dot(normed, w_in[0]), dot(normed, w_in[1]))
        square = pre * pre
        bent = jnp.tanh(ROOT * pre * (1.0 + CUBE * square))
        active = 0.5 * pre * (1.0 + bent)
        slope[rows, :] = 0.5 * (1.0 + bent) + (0.5 * ROOT) * pre * (1.0 - bent * bent) * (
            1.0 + 3.0 * CUBE * square
        )
        active_low = active.astype(BF)
        act[rows, :] = active_low
        down = jnp.where(chosen > 0.5, dot(active_low, w_down[0]), dot(active_low, w_down[1]))
        part_a[rows, :] = down.astype(BF)

    def end_layer(m):
        combined = ffn_scatter[m].finish()
        own = own_rows(m)
        out_hidden[own, :] = (middle[own, :] + gate[own, :] * combined).astype(BF)

    def gated_grad(m):
        rows = part_rows(m)
        grad_comb[rows, :] = (gate[rows, :] * wide(grad_top[rows, :])).astype(BF)

    def experts_back(m):
        rows = part_rows(m)
        chosen, share = expert[rows, :], gate[rows, :]
        top = wide(grad_top[rows, :])
        low = grad_comb[rows, :]
        into = jnp.where(chosen > 0.5, dot_nt(low, w_down[0]), dot_nt(low, w_down[1]))
        pre_low = (into * slope[rows, :]).astype(BF)
        grad_pre[rows, :] = pre_low
        back = jnp.where(chosen > 0.5, dot_nt(pre_low, w_in[0]), dot_nt(pre_low, w_in[1]))
        grad_gate = jnp.sum(top * wide(part_a[rows, :]), axis=-1, keepdims=True)
        logit = share * (1.0 - share) * grad_gate * (2.0 * chosen - 1.0)
        small[0:1, 0:768] += jnp.sum(wide(n_ffn[rows, :]) * logit, axis=0, keepdims=True)
        part_b[rows, :] = (back + logit * router_gap()).astype(BF)
        back_scatter[m].start()

    def w_spread():
        w_gather.finish()
        for out in w_share:
            out.start()

    def w_finish():
        for arriving in w_share:
            arriving.wait()

    def middle_back(m):
        own = own_rows(m)
        grad_nffn = back_scatter[m].finish()
        values = middle[own, :]
        scale = inverse_rms(values)
        small[3:4, 0:768] += jnp.sum(grad_nffn * values * scale, axis=0, keepdims=True)
        g = grad_nffn * gain_ffn[...]
        inner = jnp.mean(g * values, axis=-1, keepdims=True)
        grad_middle = wide(grad_top[own, :]) + scale * (g - values * scale * scale * inner)
        grad_mid[kept_rows(m), :] = grad_middle
        grad_branch[own, :] = grad_middle.astype(BF)
        branch_gather[m].start()

    def attention_back(m):
        rows = part_rows(m)
        branch_gather[m].finish()
        grad_att = dot_nt(grad_branch[rows, :], w_out[...]).astype(BF)
        for h in range(3):
            grad_heads[h, rows, :] = grad_att[:, h * 64 : (h + 1) * 64]
        for s in range(m * ROWS // 128, (m + 1) * ROWS // 128):
            rows = pl.ds(s * 128, 128)
            for h in range(3):
                weights = probs[3 * s + h]
                grad_att = grad_heads[h, rows, :]
                grad_w = dot_nt(grad_att, heads[6 + h, rows, :])
                mean = jnp.sum(weights * grad_w, axis=-1, keepdims=True)
                low = (weights * (grad_w - mean)).astype(BF)
                table_sums[h] += wide(low)
                at = h * 64
                grad_proj[rows, at : at + 64] = (0.125 * dot(low, heads[3 + h, rows, :])).astype(BF)
                at = 192 + h * 64
                grad_proj[rows, at : at + 64] = (0.125 * dot_tn(low, heads[h, rows, :])).astype(BF)
                at = 384 + h * 64
                grad_proj[rows, at : at + 64] = dot_tn(weights.astype(BF), grad_att).astype(BF)
        rows = part_rows(m)
        part_c[rows, :] = dot(grad_proj[rows, :], w_qkv[...]).astype(BF)
        attn_scatter[m].start()

    def input_back(m):
        own = own_rows(m)
        grad_nattn = attn_scatter[m].finish()
        values = wide(x_all[own, :])
        scale = inverse_rms(values)
        small[2:3, 0:768] += jnp.sum(grad_nattn * values * scale, axis=0, keepdims=True)
        q = grad_nattn * gain_attn[...]
        inner = jnp.mean(q * values, axis=-1, keepdims=True)
        out_input[own, :] = (
            grad_mid[kept_rows(m), :] + scale * (q - values * scale * scale * inner)
        ).astype(BF)

    def expert_grads(base, left, right):
        for e in range(2):
            mask = expert[...] if e == 0 else 1.0 - expert[...]
            masked = right[...] * mask.astype(BF)
            ffn_grads[pl.ds(base + e * 768, 768), :] = dot_tn(left[...], masked).astype(BF)

    def down_grads():
        expert_grads(1536, act, grad_comb)
        down_sum.pair_start()

    def in_grads():
        expert_grads(0, n_ffn, grad_pre)
        in_sum.pair_start()

    def attention_grads():
        attn_grads[0:576, :] = dot_tn(grad_proj[...], n_attn[...]).astype(BF)
        attn_grads[576:768, :] = dot_tn(att_all[t], grad_branch[...]).astype(BF)
        attn_sum.pair_start()

    def small_z_start():
        small[1:2, 0:768] = -small[0:1, 0:768]
        small_z[t] = small[:, 0:768]
        for out in small_over_z:
            out.start()

    def table():
        def add_table(b, carry):
            hit = buckets[...] == b
            for h in range(3):
                table_rows[h, pl.ds(b, 1), :] = jnp.sum(
                    jnp.where(hit, table_sums[h], 0.0), axis=0, keepdims=True
                )
            return carry

        lax.fori_loop(0, 32, add_table, 0)
        for h in range(3):
            line = lax.dot_general(
                jnp.ones((8, 128), F32),
                table_rows[h],
                (((1,), (1,)), ((), ())),
                precision=lax.Precision.HIGHEST,
                preferred_element_type=F32,
            )
            small[h : h + 1, 768:896] = line[0:1, :]

    def small_y_start():
        for arriving in small_over_z:
            arriving.wait()
        small_y[y, :, 0:768] = ((small_z[0] + small_z[1]) + small_z[2]) + small_z[3]
        small_y[y, :, 768:896] = small[:, 768:896]
        for out in small_over_y:
            out.start()

    def small_xc_start():
        for arriving in small_over_y:
            arriving.wait()
        small_xc[spot] = ((small_y[0] + small_y[1]) + small_y[2]) + small_y[3]
        for out in small_over_xc:
            out.start()

    def small_s_start():
        for arriving in small_over_xc:
            arriving.wait()
        total = ((small_xc[0] + small_xc[1]) + small_xc[2]) + small_xc[3]
        out_small[...] = total
        small_s[0] = total[:, 768:896]
        small_over_s.start()

    def small_end():
        small_over_s.wait()
        out_small[:, 768:896] = small_s[0] + small_s[1]

    def keep_all():
        for kept in (keep_hidden, keep_input, keep_in, keep_down, keep_attn):
            kept.wait()

    pl.semaphore_wait(barrier, len(mates))
    w_gather.start()
    opening = links.pending

    @pl.when(section == 0)
    def _():
        links.pending = list(opening)

        def middle_up(m):
            experts(m)
            ffn_scatter[m].start()

        def pass_on(m):
            end_layer(m)
            onward[m].start()
            hidden_gather[m].start()

        load_embedded.wait()
        attention(0)
        w_spread()
        attention(1)
        load_in.wait()
        load_down.wait()
        w_finish()
        middle_up(0)
        middle_up(1)
        pass_on(0)
        pass_on(1)
        for m in parts:
            returned[m].wait()
            top_gather[m].start()
        top_gather[0].finish()
        gated_grad(0)
        experts_back(0)
        top_gather[1].finish()
        gated_grad(1)
        down_grads()
        experts_back(1)
        in_grads()
        down_sum.pair_finish()
        middle_back(0)
        in_sum.pair_finish()
        middle_back(1)
        down_sum.relay()
        attention_back(0)
        in_sum.relay()
        attention_back(1)
        attention_grads()
        down_sum.cross_start()
        table()
        input_back(0)
        input_gather[0].start()
        attn_sum.pair_finish()
        input_back(1)
        input_gather[1].start()
        in_sum.cross_start()
        for m in parts:
            hidden_gather[m].finish()
        keep_hidden.start()
        small_z_start()
        down_sum.cross_finish()
        small_y_start()
        attn_sum.cross_start()
        in_sum.cross_finish()
        down_sum.forward()
        small_xc_start()
        attn_sum.cross_finish()
        in_sum.forward()
        small_s_start()
        down_sum.share()
        in_sum.share()
        attn_sum.share()
        for m in parts:
            input_gather[m].finish()
        keep_input.start()
        small_end()
        down_sum.finish()
        keep_down.start()
        in_sum.finish()
        keep_in.start()
        attn_sum.finish()
        keep_attn.start()
        keep_all()
        links.drain()

    @pl.when(section == 1)
    def _():
        links.pending = list(opening)
        load_cotangent.wait()
        load_in.wait()
        load_down.wait()
        w_spread()
        w_finish()
        for m in parts:
            onward[m].wait()
            x_gather[m].start()
        for m in parts:
            x_gather[m].finish()
            attention(m)
        for m in parts:
            experts(m)
            gated_grad(m)
            experts_back(m)
        for m in parts:
            middle_back(m)
        for m in parts:
            attention_back(m)
        for m in parts:
            input_back(m)
            returned[m].start()
        for m in parts:
            input_gather[m].start()
            ffn_scatter[m].start()
        down_grads()
        in_grads()
        attention_grads()
        down_sum.pair_finish()
        in_sum.pair_finish()
        attn_sum.pair_finish()
        small_z_start()
        table()
        for m in parts:
            end_layer(m)
            hidden_gather[m].start()
        small_y_start()
        small_xc_start()
        small_s_start()
        for step in ("relay", "cross_start", "cross_finish", "forward", "share", "finish"):
            for unit in (down_sum, in_sum, attn_sum):
                getattr(unit, step)()
        for m in parts:
            hidden_gather[m].finish()
            input_gather[m].finish()
        for kept in (keep_hidden, keep_input, keep_in, keep_down, keep_attn):
            kept.start()
        small_end()
        keep_all()
        links.drain()


def widen(hidden, grad_input, ffn_in, ffn_down, attn_qkv, attn_out, small, *outs):
    for low, out in zip((hidden, grad_input, ffn_in, ffn_down, attn_qkv, attn_out), outs):
        out[...] = wide(low[...])
    out_router, out_gain_attn, out_gain_ffn, out_table = outs[6:]

    @pl.when(pl.program_id(0) == 0)
    def _():
        out_router[...] = small[0:2, 0:768]
        out_gain_attn[...] = small[2:3, 0:768]
        out_gain_ffn[...] = small[3:4, 0:768]
        out_table[...] = small[0:3, 768:800]


def shards(
    embedded,
    expert_index,
    buckets,
    rel_bias,
    gain_attn,
    w_qkv,
    w_out,
    gain_ffn,
    w_router,
    w_in,
    w_down,
    cotangent,
):
    vmem, smem = pl.BlockSpec(memory_space=pltpu.VMEM), pl.BlockSpec(memory_space=pltpu.SMEM)
    anywhere = pl.BlockSpec(memory_space=pl.ANY)
    hidden, grad_input, ffn, attn, small = pl.pallas_call(
        kernel,
        out_shape=[
            jax.ShapeDtypeStruct((512, 768), BF),
            jax.ShapeDtypeStruct((512, 768), BF),
            jax.ShapeDtypeStruct((3072, 768), BF),
            jax.ShapeDtypeStruct((768, 768), BF),
            jax.ShapeDtypeStruct((8, 896), F32),
        ],
        in_specs=[anywhere, vmem, vmem, smem] + [vmem] * 5 + [anywhere] * 3,
        out_specs=[anywhere] * 4 + [vmem],
        scratch_shapes=[
            pltpu.VMEM((512, 768), BF),
            pltpu.VMEM((512, 768), BF),
            pltpu.VMEM((3072, 768), BF),
            pltpu.VMEM((768, 768), BF),
            pltpu.VMEM((512, 768), BF),
            pltpu.VMEM((512, 768), BF),
            pltpu.VMEM((9, 512, 64), BF),
            pltpu.VMEM((12, 128, 128), F32),
            pltpu.VMEM((3, 128, 128), F32),
            pltpu.VMEM((3, 128, 128), F32),
            pltpu.VMEM((4, 512, 192), BF),
            pltpu.VMEM((4, 192, 768), BF),
            pltpu.VMEM((512, 768), F32),
            pltpu.VMEM((512, 768), BF),
            pltpu.VMEM((512, 1), F32),
            pltpu.VMEM((512, 1), F32),
            pltpu.VMEM((512, 768), BF),
            pltpu.VMEM((512, 768), F32),
            pltpu.VMEM((512, 768), BF),
            pltpu.VMEM((512, 768), BF),
            pltpu.VMEM((512, 768), BF),
            pltpu.VMEM((3, MB, 3, OWN, 768), BF),
            pltpu.VMEM((512, 768), BF),
            pltpu.VMEM((512, 768), BF),
            pltpu.VMEM((512, 768), BF),
            pltpu.VMEM((512, 768), BF),
            pltpu.VMEM((128, 768), F32),
            pltpu.VMEM((3, 512, 64), BF),
            pltpu.VMEM((512, 576), BF),
            pltpu.VMEM((3, 128, 128), F32),
            pltpu.VMEM((3072, 768), BF),
            pltpu.VMEM((768, 768), BF),
            pltpu.VMEM((2, 768, 768), BF),
            pltpu.VMEM((384, 768), BF),
            pltpu.VMEM((2, 6, 96, 768), BF),
            pltpu.VMEM((3, 96, 768), BF),
            pltpu.VMEM((2, 2, 96, 768), BF),
            pltpu.VMEM((2, 2, 192, 768), BF),
            pltpu.VMEM((2, 96, 768), BF),
            pltpu.VMEM((8, 896), F32),
            pltpu.VMEM((4, 8, 768), F32),
            pltpu.VMEM((4, 8, 896), F32),
            pltpu.VMEM((4, 8, 896), F32),
            pltpu.VMEM((2, 8, 128), F32),
            pltpu.VMEM((2, 768, 768), BF),
            pltpu.VMEM((2, 768, 768), BF),
            pltpu.SemaphoreType.DMA((9,)),
            pltpu.SemaphoreType.DMA((COPIES,)),
            pltpu.SemaphoreType.DMA((COPIES,)),
        ],
        compiler_params=pltpu.CompilerParams(
            collective_id=0, has_side_effects=True, vmem_limit_bytes=60 * 1024 * 1024
        ),
    )(
        embedded,
        expert_index.reshape(1, 512),
        buckets,
        rel_bias.T,
        gain_attn,
        jnp.transpose(w_qkv[0], (0, 2, 1)).reshape(576, 768),
        w_out[0],
        gain_ffn,
        w_router[0].T,
        w_in[0],
        w_down[0],
        cotangent,
    )
    rows = lambda size, start=0: pl.BlockSpec((size, 768), lambda i: (i + start, 0))
    whole = lambda *dims: pl.BlockSpec(dims, lambda i: (0,) * len(dims))
    shape = lambda *dims: jax.ShapeDtypeStruct(dims, F32)
    results = pl.pallas_call(
        widen,
        grid=(4,),
        in_specs=[
            rows(128),
            rows(128),
            rows(384),
            rows(384, 4),
            rows(144),
            rows(48, 12),
            whole(8, 896),
        ],
        out_specs=[
            rows(128),
            rows(128),
            rows(384),
            rows(384),
            rows(144),
            rows(48),
            whole(2, 768),
            whole(1, 768),
            whole(1, 768),
            whole(3, 32),
        ],
        out_shape=[
            shape(512, 768),
            shape(512, 768),
            shape(1536, 768),
            shape(1536, 768),
            shape(576, 768),
            shape(192, 768),
            shape(2, 768),
            shape(1, 768),
            shape(1, 768),
            shape(3, 32),
        ],
        compiler_params=pltpu.CompilerParams(vmem_limit_bytes=60 * 1024 * 1024),
    )(hidden, grad_input, ffn, ffn, attn, attn, small)
    hidden, grad_input, grad_in, grad_down, grad_qkv, grad_out = results[:6]
    grad_router, grad_gain_attn, grad_gain_ffn, grad_table = results[6:]
    return (
        hidden[None],
        grad_input[None],
        grad_table.T,
        grad_gain_attn,
        jnp.transpose(grad_qkv.reshape(1, 3, 192, 768), (0, 1, 3, 2)),
        grad_out[None],
        grad_gain_ffn,
        grad_router.T[None],
        grad_in.reshape(1, 2, 768, 768),
        grad_down.reshape(1, 2, 768, 768),
    )


def solution(mesh):
    in_specs = (
        P("dp", None),
        P("section", "dp", None),
        P(),
        P(None, "tensor"),
        P("section", None),
        P("section", None, None, "tensor"),
        P("section", "tensor", None),
        P("section", None),
        P("section", None, None),
        P("section", None, None, "tensor"),
        P("section", None, "tensor", None),
        P("dp", None),
    )
    out_specs = (
        P("section", "dp", None),
        P("section", "dp", None),
        P(None, "tensor"),
        P("section", None),
        P("section", None, None, "tensor"),
        P("section", "tensor", None),
        P("section", None),
        P("section", None, None),
        P("section", None, None, "tensor"),
        P("section", None, "tensor", None),
    )
    return jax.shard_map(shards, mesh=mesh, in_specs=in_specs, out_specs=out_specs, check_vma=False)
```

```python
import functools

import jax
import jax.numpy as jnp
from jax import lax
from jax.experimental import pallas as pl
from jax.experimental.pallas import tpu as pltpu
from jax.sharding import PartitionSpec as P

BF = jnp.bfloat16
F32 = jnp.float32
EPS = 1e-06
ROOT = 0.7978845608028654
CUBE = 0.044715
MB = 2
ROWS = 512 // MB
OWN = 128 // MB
HALF = OWN // 2
COPIES = 64 + 32 * MB


def dot(a, b):
    return jnp.dot(a, b, preferred_element_type=F32)


def dot_nt(a, b):
    return lax.dot_general(a, b, (((1,), (1,)), ((), ())), preferred_element_type=F32)


def dot_tn(a, b):
    return lax.dot_general(a, b, (((0,), (0,)), ((), ())), preferred_element_type=F32)


def wide(v):
    return v.astype(F32)


def inverse_rms(values):
    return lax.rsqrt(jnp.mean(values * values, axis=-1, keepdims=True) + EPS)


class Links:
    def __init__(self, send_sems, recv_sems):
        self.send_sems, self.recv_sems = send_sems, recv_sems
        self.used = 0
        self.pending = []

    def copy(self, src, dst, device, landing=None):
        return Copy(self, src, dst, device, landing)

    def drain(self):
        for out in self.pending:
            out.wait_send()
        self.pending = []


class Copy:
    def __init__(self, links, src, dst, device, landing):
        slot = links.used
        links.used += 1
        make = functools.partial(
            pltpu.make_async_remote_copy,
            src_ref=src,
            send_sem=links.send_sems.at[slot],
            recv_sem=links.recv_sems.at[slot],
            device_id=device,
            device_id_type=pl.DeviceIdType.MESH,
        )
        self.links = links
        self.out = make(dst_ref=dst)
        self.arriving = self.out if landing is None else make(dst_ref=landing)

    def start(self):
        self.out.start()
        self.links.pending.append(self.out)

    def wait(self):
        self.arriving.wait_recv()


class Gather:
    def __init__(self, links, at, right, left):
        copy = links.copy
        self.a_right = copy(at(0, 0), at(0, 0), right, at(3, 0))
        self.b_left = copy(at(0, 1), at(0, 1), left, at(1, 1))
        self.b_right = copy(at(0, 1), at(0, 1), right, at(3, 1))
        self.a_left = copy(at(0, 0), at(0, 0), left, at(1, 0))
        self.a_far = copy(at(3, 0), at(3, 0), right, at(2, 0))
        self.b_far = copy(at(1, 1), at(1, 1), left, at(2, 1))

    def start(self):
        for first in (self.a_right, self.b_left, self.b_right, self.a_left):
            first.start()

    def forward(self):
        self.a_right.wait()
        self.a_far.start()
        self.b_left.wait()
        self.b_far.start()

    def finish(self):
        for arriving in (self.b_right, self.a_left, self.a_far, self.b_far):
            arriving.wait()


class Scatter:
    def __init__(self, links, part, landed, summed, right, left):
        self.part, self.landed, self.summed = part, landed, summed
        copy = links.copy
        self.far_a = copy(part(2, 0), landed.at[0], right)
        self.far_b = copy(part(2, 1), landed.at[1], left)
        self.near_b = copy(part(1, 1), landed.at[2], right)
        self.near_a = copy(part(3, 0), landed.at[3], left)
        self.sum_a = copy(summed.at[0], landed.at[4], right)
        self.sum_b = copy(summed.at[1], landed.at[5], left)

    def start(self):
        for first in (self.far_a, self.far_b, self.near_b, self.near_a):
            first.start()

    def relay(self):
        part, landed, summed = self.part, self.landed, self.summed
        self.far_a.wait()
        summed[0] = (wide(landed[0]) + wide(part(1, 0)[...])).astype(BF)
        self.sum_a.start()
        self.far_b.wait()
        summed[1] = (wide(landed[1]) + wide(part(3, 1)[...])).astype(BF)
        self.sum_b.start()

    def finish(self):
        for arriving in (self.near_b, self.near_a, self.sum_a, self.sum_b):
            arriving.wait()
        landed, part = self.landed, self.part
        top = wide(part(0, 0)[...]) + wide(landed[3]) + wide(landed[4])
        bottom = wide(part(0, 1)[...]) + wide(landed[2]) + wide(landed[5])
        return jnp.concatenate([top, bottom], axis=0)


class DirectGather:
    def __init__(self, links, at, device):
        self.copies = [
            links.copy(at(0), at(0), device(k), at((4 - k) % 4)) for k in (2, 1, 3)
        ]

    def start(self):
        for out in self.copies:
            out.start()

    def forward(self):
        pass

    def finish(self):
        for arriving in self.copies:
            arriving.wait()


class DirectScatter:
    def __init__(self, links, part, landed, device):
        self.part, self.landed = part, landed
        self.copies = [
            links.copy(part(k), landed.at[i], device(k)) for i, k in enumerate((2, 1, 3))
        ]

    def start(self):
        for out in self.copies:
            out.start()

    def relay(self):
        pass

    def finish(self):
        for arriving in self.copies:
            arriving.wait()
        landed = self.landed
        return ((wide(self.part(0)[...]) + wide(landed[0])) + wide(landed[1])) + wide(landed[2])


class Reduce:
    def __init__(self, links, place, mates, grads, result, base, rows, pair, landed, summed, cross):
        (y, c), (ring, x_mate, c_mate) = place, mates
        self.grads, self.result, self.pair, self.cross = grads, result, pair, cross
        self.half, eighth, sixteenth = rows // 2, rows // 8, rows // 16
        self.mine = pl.multiple_of(base + c * self.half, 16)

        def at(ref):
            def view(k, half=None):
                start = self.mine + ((y + k) % 4) * eighth
                if half is None:
                    return ref.at[pl.ds(pl.multiple_of(start, 16), eighth)]
                start = start + half * sixteenth
                return ref.at[pl.ds(pl.multiple_of(start, 16), sixteenth)]

            return view

        theirs = pl.ds(pl.multiple_of(base + (1 - c) * self.half, 16), self.half)
        mine = pl.ds(self.mine, self.half)
        self.here = pl.ds(pl.multiple_of(self.mine + y * eighth, 16), eighth)
        self.paired = links.copy(grads.at[theirs], pair, c_mate)
        if summed is None:
            self.scatter = DirectScatter(links, at(grads), landed, ring)
        else:
            self.scatter = Scatter(links, at(grads), landed, summed, ring(1), ring(3))
        self.crossed = links.copy(cross.at[0], cross.at[1], x_mate)
        if summed is None:
            self.gather = DirectGather(links, at(result), ring)
        else:
            self.gather = Gather(links, at(result), ring(1), ring(3))
        self.shared = links.copy(result.at[mine], result.at[mine], c_mate, result.at[theirs])

    def pair_start(self):
        self.paired.start()

    def pair_finish(self):
        self.paired.wait()
        step = 96

        def add(i, carry):
            mine = pl.ds(pl.multiple_of(self.mine + i * step, 16), step)
            self.grads[mine, :] = (
                wide(self.grads[mine, :]) + wide(self.pair[pl.ds(i * step, step), :])
            ).astype(BF)
            return carry

        lax.fori_loop(0, self.half // step, add, 0)
        self.scatter.start()

    def relay(self):
        self.scatter.relay()

    def cross_start(self):
        self.cross[0] = self.scatter.finish().astype(BF)
        self.crossed.start()

    def cross_finish(self):
        self.crossed.wait()
        self.result[self.here, :] = (wide(self.cross[0]) + wide(self.cross[1])).astype(BF)
        self.gather.start()

    def forward(self):
        self.gather.forward()

    def share(self):
        self.gather.finish()
        self.shared.start()

    def finish(self):
        self.shared.wait()


def kernel(
    embedded,
    expert_index,
    buckets,
    rel_bias,
    gain_attn,
    w_qkv_hbm,
    w_out_hbm,
    gain_ffn,
    router,
    w_in_hbm,
    w_down_hbm,
    cotangent,
    hidden_hbm,
    input_hbm,
    ffn_hbm,
    attn_hbm,
    out_small,
    out_hidden,
    out_input,
    out_ffn,
    out_attn,
    x_all,
    n_attn,
    heads,
    probs,
    bias,
    table_sums,
    att_all,
    w_out_all,
    middle,
    n_ffn,
    gate,
    expert,
    act,
    slope,
    part_a,
    part_b,
    part_c,
    landed_z,
    grad_top,
    grad_comb,
    grad_pre,
    grad_branch,
    grad_mid,
    grad_heads,
    grad_proj,
    table_rows,
    ffn_grads,
    attn_grads,
    ffn_pair,
    attn_pair,
    ffn_landed,
    attn_landed,
    ffn_summed,
    ffn_cross,
    attn_cross,
    small,
    small_z,
    small_y,
    small_xc,
    small_s,
    w_qkv,
    w_in,
    w_down,
    load_sems,
    send_sems,
    recv_sems,
):
    section, t, d = lax.axis_index("section"), lax.axis_index("tensor"), lax.axis_index("dp")
    y, xl, c = d // 4, (d // 2) % 2, d % 2
    ztx = lambda k: {"tensor": (t + k) % 4}
    ydx = lambda k: {"dp": (d + 4 * k) % 16}
    x_mate, c_mate = {"dp": d + 2 - 4 * xl}, {"dp": d + 1 - 2 * c}
    xc_mate = {"dp": d + 2 - 4 * xl + 1 - 2 * c}
    s_mate = {"section": 1 - section}
    links = Links(send_sems, recv_sems)

    keep_hidden = pltpu.make_async_copy(out_hidden, hidden_hbm, load_sems.at[4])
    keep_input = pltpu.make_async_copy(out_input, input_hbm, load_sems.at[5])
    keep_in, keep_down = [
        pltpu.make_async_copy(
            out_ffn.at[pl.ds(i * 1536, 1536)], ffn_hbm.at[pl.ds(i * 1536, 1536)], load_sems.at[6 + i]
        )
        for i in range(2)
    ]
    keep_attn = pltpu.make_async_copy(out_attn, attn_hbm, load_sems.at[8])
    load_in = pltpu.make_async_copy(w_in_hbm, w_in, load_sems.at[0])
    load_down = pltpu.make_async_copy(w_down_hbm, w_down, load_sems.at[1])
    load_qkv = pltpu.make_async_copy(w_qkv_hbm, w_qkv, load_sems.at[9])
    load_out = pltpu.make_async_copy(w_out_hbm, w_out_all.at[t], load_sems.at[10])
    load_embedded = pltpu.make_async_copy(embedded, x_all, load_sems.at[2])
    load_cotangent = pltpu.make_async_copy(cotangent, grad_top, load_sems.at[3])

    load_out.start()
    load_qkv.start()

    @pl.when(section == 0)
    def _():
        load_embedded.start()

    @pl.when(section == 1)
    def _():
        load_cotangent.start()

    load_in.start()
    load_down.start()
    barrier = pltpu.get_barrier_semaphore()
    mates = [ztx(1), ztx(2), ztx(3), ydx(1), ydx(2), ydx(3), x_mate, c_mate, xc_mate, s_mate]
    for mate in mates:
        pl.semaphore_signal(barrier, inc=1, device_id=mate, device_id_type=pl.DeviceIdType.MESH)

    def part_rows(m):
        return pl.ds(m * ROWS, ROWS)

    def own_rows(m):
        return pl.ds(pl.multiple_of(m * ROWS + t * OWN, OWN), OWN)

    def kept_rows(m):
        return pl.ds(m * OWN, OWN)

    def blocks(ref, m):
        return lambda k: ref.at[
            pl.ds(pl.multiple_of(m * ROWS + ((t + k) % 4) * OWN, OWN), OWN)
        ]

    def z_gather(at):
        return DirectGather(links, at, ztx)

    def z_scatter(part, kind, m):
        return DirectScatter(links, blocks(part, m), landed_z.at[kind, m], ztx)

    parts = range(MB)
    w_half = lambda k: w_out_all.at[(t + k) % 4, pl.ds(pl.multiple_of(c * 96, 16), 96)]
    w_rest = lambda k: w_out_all.at[(t + k) % 4, pl.ds(pl.multiple_of(96 - c * 96, 16), 96)]
    w_gather = z_gather(w_half)
    w_share = [links.copy(w_half(k), w_half(k), c_mate, w_rest(k)) for k in (1, 2, 3)]
    x_gather = [z_gather(blocks(x_all, m)) for m in parts]
    att_gather = [
        z_gather(lambda k, m=m: att_all.at[(t + k) % 4, pl.ds(m * ROWS, ROWS)])
        for m in parts
    ]
    ffn_scatter = [z_scatter(part_a, 0, m) for m in parts]
    hidden_gather = [z_gather(blocks(out_hidden, m)) for m in parts]
    top_gather = [z_gather(blocks(grad_top, m)) for m in parts]
    back_scatter = [z_scatter(part_b, 1, m) for m in parts]
    branch_gather = [z_gather(blocks(grad_branch, m)) for m in parts]
    attn_scatter = [z_scatter(part_c, 2, m) for m in parts]
    input_gather = [z_gather(blocks(out_input, m)) for m in parts]
    onward = [
        links.copy(out_hidden.at[own_rows(m)], x_all.at[own_rows(m)], s_mate) for m in parts
    ]
    returned = [
        links.copy(out_input.at[own_rows(m)], grad_top.at[own_rows(m)], s_mate) for m in parts
    ]
    place, ring = (y, c), (ydx, x_mate, c_mate)
    down_sum, in_sum = [
        Reduce(
            links,
            place,
            ring,
            ffn_grads,
            out_ffn,
            1536 * (1 - i),
            1536,
            ffn_pair.at[i],
            ffn_landed.at[i],
            ffn_summed.at[i],
            ffn_cross.at[i],
        )
        for i in range(2)
    ]
    attn_sum = Reduce(
        links,
        place,
        ring,
        attn_grads,
        out_attn,
        0,
        768,
        attn_pair,
        attn_landed,
        None,
        attn_cross,
    )
    small_over_z = [
        links.copy(small.at[:, 0:768], small_z.at[t], ztx(k), small_z.at[(t + 4 - k) % 4])
        for k in (1, 2, 3)
    ]
    small_over_y = [
        links.copy(small_y.at[y], small_y.at[y], ydx(k), small_y.at[(y + 4 - k) % 4])
        for k in (1, 2, 3)
    ]
    spot = 2 * xl + c
    small_over_xc = [
        links.copy(small_xc.at[spot], small_xc.at[spot], mate, small_xc.at[source])
        for mate, source in (
            (x_mate, 2 * (1 - xl) + c),
            (c_mate, 2 * xl + 1 - c),
            (xc_mate, 2 * (1 - xl) + 1 - c),
        )
    ]
    small_over_s = links.copy(small_s.at[0], small_s.at[1], s_mate)

    is_first = (expert_index[...] == 0).astype(F32)
    expert[...] = jnp.broadcast_to(is_first, (8, 512)).T[:, 0:1]
    small[...] = jnp.zeros_like(small)
    table_sums[...] = jnp.zeros_like(table_sums)
    bias[...] = jnp.zeros_like(bias)
    table_rows[...] = jnp.zeros_like(table_rows)

    def add_bias(b, carry):
        hit = buckets[...] == b
        for h in range(3):
            bias[h] = jnp.where(hit, rel_bias[h, b], bias[h])
        return carry

    lax.fori_loop(0, 32, add_bias, 0)

    def router_gap():
        both = wide(router[...])
        return both[0:1, :] - both[1:2, :]

    def attention(m):
        rows = part_rows(m)
        values = wide(x_all[rows, :])
        normed = (values * inverse_rms(values) * gain_attn[...]).astype(BF)
        n_attn[rows, :] = normed
        projected = dot_nt(normed, w_qkv[...]).astype(BF)
        for i in range(9):
            heads[i, rows, :] = projected[:, i * 64 : (i + 1) * 64]
        for s in range(m * ROWS // 128, (m + 1) * ROWS // 128):
            rows = pl.ds(s * 128, 128)
            for h in range(3):
                scores = dot_nt(heads[h, rows, :], heads[3 + h, rows, :]) * 0.125 + bias[h]
                powers = jnp.exp(scores - jnp.max(scores, axis=-1, keepdims=True))
                weights = powers * (1.0 / jnp.sum(powers, axis=-1, keepdims=True))
                probs[3 * s + h] = weights
                att_all[t, rows, h * 64 : (h + 1) * 64] = dot(
                    weights.astype(BF), heads[6 + h, rows, :]
                ).astype(BF)
        att_gather[m].start()

    def experts(m):
        rows = part_rows(m)
        att_gather[m].finish()
        total = wide(x_all[rows, :])
        for source in range(4):
            total = total + dot(att_all[source, rows, :], w_out_all[source])
        middle[rows, :] = total
        normed = (total * inverse_rms(total) * gain_ffn[...]).astype(BF)
        n_ffn[rows, :] = normed
        chosen = expert[rows, :]
        gap = jnp.sum(wide(normed) * router_gap(), axis=-1, keepdims=True)
        gate[rows, :] = 1.0 / (1.0 + jnp.exp(jnp.where(chosen > 0.5, -gap, gap)))
        pre = jnp.where(chosen > 0.5, dot(normed, w_in[0]), dot(normed, w_in[1]))
        square = pre * pre
        bent = jnp.tanh(ROOT * pre * (1.0 + CUBE * square))
        active = 0.5 * pre * (1.0 + bent)
        slope[rows, :] = 0.5 * (1.0 + bent) + (0.5 * ROOT) * pre * (1.0 - bent * bent) * (
            1.0 + 3.0 * CUBE * square
        )
        active_low = active.astype(BF)
        act[rows, :] = active_low
        down = jnp.where(chosen > 0.5, dot(active_low, w_down[0]), dot(active_low, w_down[1]))
        part_a[rows, :] = down.astype(BF)

    def end_layer(m):
        combined = ffn_scatter[m].finish()
        own = own_rows(m)
        out_hidden[own, :] = (middle[own, :] + gate[own, :] * combined).astype(BF)

    def gated_grad(m):
        rows = part_rows(m)
        grad_comb[rows, :] = (gate[rows, :] * wide(grad_top[rows, :])).astype(BF)

    def experts_back(m):
        rows = part_rows(m)
        chosen, share = expert[rows, :], gate[rows, :]
        top = wide(grad_top[rows, :])
        low = grad_comb[rows, :]
        into = jnp.where(chosen > 0.5, dot_nt(low, w_down[0]), dot_nt(low, w_down[1]))
        pre_low = (into * slope[rows, :]).astype(BF)
        grad_pre[rows, :] = pre_low
        back = jnp.where(chosen > 0.5, dot_nt(pre_low, w_in[0]), dot_nt(pre_low, w_in[1]))
        grad_gate = jnp.sum(top * wide(part_a[rows, :]), axis=-1, keepdims=True)
        logit = share * (1.0 - share) * grad_gate * (2.0 * chosen - 1.0)
        small[0:1, 0:768] += jnp.sum(wide(n_ffn[rows, :]) * logit, axis=0, keepdims=True)
        part_b[rows, :] = (back + logit * router_gap()).astype(BF)
        back_scatter[m].start()

    def w_spread():
        w_gather.finish()
        for out in w_share:
            out.start()

    def w_finish():
        for arriving in w_share:
            arriving.wait()

    def middle_back(m):
        own = own_rows(m)
        grad_nffn = back_scatter[m].finish()
        values = middle[own, :]
        scale = inverse_rms(values)
        small[3:4, 0:768] += jnp.sum(grad_nffn * values * scale, axis=0, keepdims=True)
        g = grad_nffn * gain_ffn[...]
        inner = jnp.mean(g * values, axis=-1, keepdims=True)
        grad_middle = wide(grad_top[own, :]) + scale * (g - values * scale * scale * inner)
        grad_mid[kept_rows(m), :] = grad_middle
        grad_branch[own, :] = grad_middle.astype(BF)
        branch_gather[m].start()

    def attention_back(m):
        rows = part_rows(m)
        branch_gather[m].finish()
        grad_att = dot_nt(grad_branch[rows, :], w_out_all[t]).astype(BF)
        for h in range(3):
            grad_heads[h, rows, :] = grad_att[:, h * 64 : (h + 1) * 64]
        for s in range(m * ROWS // 128, (m + 1) * ROWS // 128):
            rows = pl.ds(s * 128, 128)
            for h in range(3):
                weights = probs[3 * s + h]
                grad_att = grad_heads[h, rows, :]
                grad_w = dot_nt(grad_att, heads[6 + h, rows, :])
                mean = jnp.sum(weights * grad_w, axis=-1, keepdims=True)
                low = (weights * (grad_w - mean)).astype(BF)
                table_sums[h] += wide(low)
                at = h * 64
                grad_proj[rows, at : at + 64] = (0.125 * dot(low, heads[3 + h, rows, :])).astype(BF)
                at = 192 + h * 64
                grad_proj[rows, at : at + 64] = (0.125 * dot_tn(low, heads[h, rows, :])).astype(BF)
                at = 384 + h * 64
                grad_proj[rows, at : at + 64] = dot_tn(weights.astype(BF), grad_att).astype(BF)
        rows = part_rows(m)
        part_c[rows, :] = dot(grad_proj[rows, :], w_qkv[...]).astype(BF)
        attn_scatter[m].start()

    def input_back(m):
        own = own_rows(m)
        grad_nattn = attn_scatter[m].finish()
        values = wide(x_all[own, :])
        scale = inverse_rms(values)
        small[2:3, 0:768] += jnp.sum(grad_nattn * values * scale, axis=0, keepdims=True)
        q = grad_nattn * gain_attn[...]
        inner = jnp.mean(q * values, axis=-1, keepdims=True)
        out_input[own, :] = (
            grad_mid[kept_rows(m), :] + scale * (q - values * scale * scale * inner)
        ).astype(BF)

    def expert_grads(base, left, right):
        for e in range(2):
            mask = expert[...] if e == 0 else 1.0 - expert[...]
            masked = right[...] * mask.astype(BF)
            ffn_grads[pl.ds(base + e * 768, 768), :] = dot_tn(left[...], masked).astype(BF)

    def down_grads():
        expert_grads(1536, act, grad_comb)
        down_sum.pair_start()

    def in_grads():
        expert_grads(0, n_ffn, grad_pre)
        in_sum.pair_start()

    def attention_grads():
        attn_grads[0:576, :] = dot_tn(grad_proj[...], n_attn[...]).astype(BF)
        attn_grads[576:768, :] = dot_tn(att_all[t], grad_branch[...]).astype(BF)
        attn_sum.pair_start()

    def small_z_start():
        small[1:2, 0:768] = -small[0:1, 0:768]
        small_z[t] = small[:, 0:768]
        for out in small_over_z:
            out.start()

    def table():
        def add_table(b, carry):
            hit = buckets[...] == b
            for h in range(3):
                table_rows[h, pl.ds(b, 1), :] = jnp.sum(
                    jnp.where(hit, table_sums[h], 0.0), axis=0, keepdims=True
                )
            return carry

        lax.fori_loop(0, 32, add_table, 0)
        for h in range(3):
            line = lax.dot_general(
                jnp.ones((8, 128), F32),
                table_rows[h],
                (((1,), (1,)), ((), ())),
                precision=lax.Precision.HIGHEST,
                preferred_element_type=F32,
            )
            small[h : h + 1, 768:896] = line[0:1, :]

    def small_y_start():
        for arriving in small_over_z:
            arriving.wait()
        small_y[y, :, 0:768] = ((small_z[0] + small_z[1]) + small_z[2]) + small_z[3]
        small_y[y, :, 768:896] = small[:, 768:896]
        for out in small_over_y:
            out.start()

    def small_xc_start():
        for arriving in small_over_y:
            arriving.wait()
        small_xc[spot] = ((small_y[0] + small_y[1]) + small_y[2]) + small_y[3]
        for out in small_over_xc:
            out.start()

    def small_s_start():
        for arriving in small_over_xc:
            arriving.wait()
        total = ((small_xc[0] + small_xc[1]) + small_xc[2]) + small_xc[3]
        out_small[...] = total
        small_s[0] = total[:, 768:896]
        small_over_s.start()

    def small_end():
        small_over_s.wait()
        out_small[:, 768:896] = small_s[0] + small_s[1]

    def keep_all():
        for kept in (keep_hidden, keep_input, keep_in, keep_down, keep_attn):
            kept.wait()

    load_out.wait()
    pl.semaphore_wait(barrier, len(mates))
    w_gather.start()
    opening = links.pending

    @pl.when(section == 0)
    def _():
        links.pending = list(opening)

        def middle_up(m):
            experts(m)
            ffn_scatter[m].start()

        def pass_on(m):
            end_layer(m)
            onward[m].start()
            hidden_gather[m].start()

        load_embedded.wait()
        load_qkv.wait()
        attention(0)
        attention(1)
        w_spread()
        load_in.wait()
        load_down.wait()
        w_finish()
        middle_up(0)
        middle_up(1)
        pass_on(0)
        pass_on(1)
        for m in parts:
            returned[m].wait()
            top_gather[m].start()
        top_gather[0].finish()
        gated_grad(0)
        experts_back(0)
        top_gather[1].finish()
        gated_grad(1)
        down_grads()
        experts_back(1)
        in_grads()
        down_sum.pair_finish()
        middle_back(0)
        in_sum.pair_finish()
        middle_back(1)
        down_sum.relay()
        attention_back(0)
        in_sum.relay()
        attention_back(1)
        attention_grads()
        down_sum.cross_start()
        table()
        input_back(0)
        input_gather[0].start()
        attn_sum.pair_finish()
        input_back(1)
        input_gather[1].start()
        in_sum.cross_start()
        for m in parts:
            hidden_gather[m].finish()
        keep_hidden.start()
        small_z_start()
        down_sum.cross_finish()
        small_y_start()
        attn_sum.cross_start()
        down_sum.forward()
        in_sum.cross_finish()
        small_xc_start()
        attn_sum.cross_finish()
        in_sum.forward()
        down_sum.share()
        small_s_start()
        in_sum.share()
        attn_sum.share()
        for m in parts:
            input_gather[m].finish()
        keep_input.start()
        small_end()
        down_sum.finish()
        keep_down.start()
        in_sum.finish()
        keep_in.start()
        attn_sum.finish()
        keep_attn.start()
        keep_all()
        links.drain()

    @pl.when(section == 1)
    def _():
        links.pending = list(opening)
        load_cotangent.wait()
        load_qkv.wait()
        load_in.wait()
        load_down.wait()
        w_spread()
        w_finish()
        for m in parts:
            onward[m].wait()
            x_gather[m].start()
        for m in parts:
            x_gather[m].finish()
            attention(m)
        for m in parts:
            experts(m)
            gated_grad(m)
            experts_back(m)
        for m in parts:
            middle_back(m)
        for m in parts:
            attention_back(m)
        for m in parts:
            input_back(m)
            returned[m].start()
        for m in parts:
            input_gather[m].start()
            ffn_scatter[m].start()
        down_grads()
        in_grads()
        attention_grads()
        down_sum.pair_finish()
        in_sum.pair_finish()
        attn_sum.pair_finish()
        small_z_start()
        table()
        for m in parts:
            end_layer(m)
            hidden_gather[m].start()
        small_y_start()
        small_xc_start()
        small_s_start()
        for step in ("relay", "cross_start", "cross_finish", "forward", "share", "finish"):
            for unit in (down_sum, in_sum, attn_sum):
                getattr(unit, step)()
        for m in parts:
            hidden_gather[m].finish()
            input_gather[m].finish()
        for kept in (keep_hidden, keep_input, keep_in, keep_down, keep_attn):
            kept.start()
        small_end()
        keep_all()
        links.drain()


def widen(hidden, grad_input, ffn_in, ffn_down, attn_qkv, attn_out, small, *outs):
    for low, out in zip((hidden, grad_input, ffn_in, ffn_down, attn_qkv, attn_out), outs):
        out[...] = wide(low[...])
    out_router, out_gain_attn, out_gain_ffn, out_table = outs[6:]

    @pl.when(pl.program_id(0) == 0)
    def _():
        out_router[...] = small[0:2, 0:768]
        out_gain_attn[...] = small[2:3, 0:768]
        out_gain_ffn[...] = small[3:4, 0:768]
        out_table[...] = small[0:3, 768:800]


def shards(
    embedded,
    expert_index,
    buckets,
    rel_bias,
    gain_attn,
    w_qkv,
    w_out,
    gain_ffn,
    w_router,
    w_in,
    w_down,
    cotangent,
):
    vmem, smem = pl.BlockSpec(memory_space=pltpu.VMEM), pl.BlockSpec(memory_space=pltpu.SMEM)
    anywhere = pl.BlockSpec(memory_space=pl.ANY)
    hidden, grad_input, ffn, attn, small = pl.pallas_call(
        kernel,
        out_shape=[
            jax.ShapeDtypeStruct((512, 768), BF),
            jax.ShapeDtypeStruct((512, 768), BF),
            jax.ShapeDtypeStruct((3072, 768), BF),
            jax.ShapeDtypeStruct((768, 768), BF),
            jax.ShapeDtypeStruct((8, 896), F32),
        ],
        in_specs=[anywhere, vmem, vmem, smem] + [vmem] + [anywhere] * 2 + [vmem] * 2 + [anywhere] * 3,
        out_specs=[anywhere] * 4 + [vmem],
        scratch_shapes=[
            pltpu.VMEM((512, 768), BF),
            pltpu.VMEM((512, 768), BF),
            pltpu.VMEM((3072, 768), BF),
            pltpu.VMEM((768, 768), BF),
            pltpu.VMEM((512, 768), BF),
            pltpu.VMEM((512, 768), BF),
            pltpu.VMEM((9, 512, 64), BF),
            pltpu.VMEM((12, 128, 128), F32),
            pltpu.VMEM((3, 128, 128), F32),
            pltpu.VMEM((3, 128, 128), F32),
            pltpu.VMEM((4, 512, 192), BF),
            pltpu.VMEM((4, 192, 768), BF),
            pltpu.VMEM((512, 768), F32),
            pltpu.VMEM((512, 768), BF),
            pltpu.VMEM((512, 1), F32),
            pltpu.VMEM((512, 1), F32),
            pltpu.VMEM((512, 768), BF),
            pltpu.VMEM((512, 768), F32),
            pltpu.VMEM((512, 768), BF),
            pltpu.VMEM((512, 768), BF),
            pltpu.VMEM((512, 768), BF),
            pltpu.VMEM((3, MB, 3, OWN, 768), BF),
            pltpu.VMEM((512, 768), BF),
            pltpu.VMEM((512, 768), BF),
            pltpu.VMEM((512, 768), BF),
            pltpu.VMEM((512, 768), BF),
            pltpu.VMEM((128, 768), F32),
            pltpu.VMEM((3, 512, 64), BF),
            pltpu.VMEM((512, 576), BF),
            pltpu.VMEM((3, 128, 128), F32),
            pltpu.VMEM((3072, 768), BF),
            pltpu.VMEM((768, 768), BF),
            pltpu.VMEM((2, 768, 768), BF),
            pltpu.VMEM((384, 768), BF),
            pltpu.VMEM((2, 6, 96, 768), BF),
            pltpu.VMEM((3, 96, 768), BF),
            pltpu.VMEM((2, 2, 96, 768), BF),
            pltpu.VMEM((2, 2, 192, 768), BF),
            pltpu.VMEM((2, 96, 768), BF),
            pltpu.VMEM((8, 896), F32),
            pltpu.VMEM((4, 8, 768), F32),
            pltpu.VMEM((4, 8, 896), F32),
            pltpu.VMEM((4, 8, 896), F32),
            pltpu.VMEM((2, 8, 128), F32),
            pltpu.VMEM((576, 768), BF),
            pltpu.VMEM((2, 768, 768), BF),
            pltpu.VMEM((2, 768, 768), BF),
            pltpu.SemaphoreType.DMA((11,)),
            pltpu.SemaphoreType.DMA((COPIES,)),
            pltpu.SemaphoreType.DMA((COPIES,)),
        ],
        compiler_params=pltpu.CompilerParams(
            collective_id=0, has_side_effects=True, vmem_limit_bytes=60 * 1024 * 1024
        ),
    )(
        embedded,
        expert_index.reshape(1, 512),
        buckets,
        rel_bias.T,
        gain_attn,
        jnp.transpose(w_qkv[0], (0, 2, 1)).reshape(576, 768),
        w_out[0],
        gain_ffn,
        w_router[0].T,
        w_in[0],
        w_down[0],
        cotangent,
    )
    rows = lambda size, start=0: pl.BlockSpec((size, 768), lambda i: (i + start, 0))
    whole = lambda *dims: pl.BlockSpec(dims, lambda i: (0,) * len(dims))
    shape = lambda *dims: jax.ShapeDtypeStruct(dims, F32)
    results = pl.pallas_call(
        widen,
        grid=(4,),
        in_specs=[
            rows(128),
            rows(128),
            rows(384),
            rows(384, 4),
            rows(144),
            rows(48, 12),
            whole(8, 896),
        ],
        out_specs=[
            rows(128),
            rows(128),
            rows(384),
            rows(384),
            rows(144),
            rows(48),
            whole(2, 768),
            whole(1, 768),
            whole(1, 768),
            whole(3, 32),
        ],
        out_shape=[
            shape(512, 768),
            shape(512, 768),
            shape(1536, 768),
            shape(1536, 768),
            shape(576, 768),
            shape(192, 768),
            shape(2, 768),
            shape(1, 768),
            shape(1, 768),
            shape(3, 32),
        ],
        compiler_params=pltpu.CompilerParams(vmem_limit_bytes=60 * 1024 * 1024),
    )(hidden, grad_input, ffn, ffn, attn, attn, small)
    hidden, grad_input, grad_in, grad_down, grad_qkv, grad_out = results[:6]
    grad_router, grad_gain_attn, grad_gain_ffn, grad_table = results[6:]
    return (
        hidden[None],
        grad_input[None],
        grad_table.T,
        grad_gain_attn,
        jnp.transpose(grad_qkv.reshape(1, 3, 192, 768), (0, 1, 3, 2)),
        grad_out[None],
        grad_gain_ffn,
        grad_router.T[None],
        grad_in.reshape(1, 2, 768, 768),
        grad_down.reshape(1, 2, 768, 768),
    )


def solution(mesh):
    in_specs = (
        P("dp", None),
        P("section", "dp", None),
        P(),
        P(None, "tensor"),
        P("section", None),
        P("section", None, None, "tensor"),
        P("section", "tensor", None),
        P("section", None),
        P("section", None, None),
        P("section", None, None, "tensor"),
        P("section", None, "tensor", None),
        P("dp", None),
    )
    out_specs = (
        P("section", "dp", None),
        P("section", "dp", None),
        P(None, "tensor"),
        P("section", None),
        P("section", None, None, "tensor"),
        P("section", "tensor", None),
        P("section", None),
        P("section", None, None),
        P("section", None, None, "tensor"),
        P("section", None, "tensor", None),
    )
    return jax.shard_map(shards, mesh=mesh, in_specs=in_specs, out_specs=out_specs, check_vma=False)
```
